256 devices in a mesh: sector: 16 (over y, x), bin: 16 (over z, core).
Axes of the slice: x: 4, y: 4, z: 8, core: 2. Of those that a mesh axis runs over, the one named last changes fastest.
Arguments:
- sph_state: float32 [7, 262144], P(None, ('sector', 'bin')), as said below
- sph_dest: int32 [262144, 1], P(('sector', 'bin')), may hold values from 0 to 255; in each aligned block of 1024 rows (0 to 1023, 1024 to 2047, ...) at most 8 rows name the same one
- body_list: int32 [256, 2], P(('sector', 'bin')), may hold values from 0 to 15, all different within a row
- tile_codes: int32 [256, 2, 32], P(('sector', 'bin')), may hold values from 0 to 511, as said below
- triangles: float32 [9, 16, 65536], P(None, 'sector', 'bin'), as said below
Outputs:
- new_state: float32 [7, 524288], P(None, ('sector', 'bin'))
- body_kick: float32 [16, 6], P('sector')
The draws below stay inside these ranges and needn't reach their ends.
Inputs may be any that keep to these rules, and one draw needn't show every extreme that they name: `sph_dest`: within the spheres of one source bin no destination is named by more than 8 spheres, a bound that some block reaches. `body_list`: the 2 bodies of one bin are different. `tile_codes`: the 32 codes of one bin and intersection entry are different. `sph_state`: every radius (row 6) lies between 0.3 and 0.7. `triangles`: for every triangle, |e1 x e2|^2 is at least 0.2.
All inputs are finite; a program needn't handle non-finite values.
Results may differ from the reference program's by a relative error of at most 0.0003.
Values sent between devices are 32-bit elements; how exact they have to be, the bound alone decides.
A program may use at most 64 MiB of HBM per device.

```python
import math
import jax
import jax.numpy as jnp
import numpy as np
from jax import lax

SPH_DEV = 1024
TBLK = 4096
NPO = 32
OVL = 2
BODIES = 16
DEVROWS = 256
CAP = 8
SPHERES = 262144
SLOTS = 524288
NBTRI = 65536
STILES = 16
TTILES = 32
N_SECTOR = 16
N_BIN = 16


def draw_sph_state(key, part):
    key = jax.random.fold_in(key, 101)
    key_position, key_velocity, key_radius = jax.random.split(key, 3)
    extent = 9.0
    position = jax.random.uniform(key_position, (3, SPHERES), jnp.float32, 0.0, extent)
    velocity = jnp.clip(jax.random.normal(key_velocity, (3, SPHERES), jnp.float32), -6.0, 6.0)
    radius = jax.random.uniform(key_radius, (1, SPHERES), jnp.float32, 0.3, 0.7)
    return jnp.concatenate([position, velocity, radius], 0).astype(jnp.float32)


def draw_triangles(key, part):
    key = jax.random.fold_in(key, 202)
    key_corner, key_first, key_second = jax.random.split(key, 3)
    extent = 9.0
    grid_shape = (3, BODIES, NBTRI)
    corner = jax.random.uniform(key_corner, grid_shape, jnp.float32, 0.0, extent)
    long_low, long_high, side_span = (0.8, 1.6, 0.4)
    first_unit = jax.random.uniform(key_first, grid_shape, jnp.float32, 0.0, 1.0)
    second_unit = jax.random.uniform(key_second, grid_shape, jnp.float32, 0.0, 1.0)
    first_low = jnp.array([long_low, -side_span, -side_span], jnp.float32)[:, None, None]
    first_high = jnp.array([long_high, side_span, side_span], jnp.float32)[:, None, None]
    second_low = jnp.array([-side_span, long_low, -side_span], jnp.float32)[:, None, None]
    second_high = jnp.array([side_span, long_high, side_span], jnp.float32)[:, None, None]
    edge_one = first_low + (first_high - first_low) * first_unit
    edge_two = second_low + (second_high - second_low) * second_unit
    return jnp.concatenate([corner, corner + edge_one, corner + edge_two], 0).astype(jnp.float32)


def draw_tile_codes(key, part):
    key = jax.random.fold_in(key, 303)
    key_list = jax.random.split(key, DEVROWS * OVL)
    choices_all = jax.vmap(lambda single: jax.random.permutation(single, STILES * TTILES)[:NPO])(key_list)
    return choices_all.reshape(DEVROWS, OVL, NPO).astype(jnp.int32)


def choose_distinct(rng, rows, number_of, top, lift):
    order = jax.random.permutation(jax.random.fold_in(rng, 1), number_of)
    favour = order
    for power in range(3):
        favour = favour * favour // number_of
    favour = favour * lift // number_of
    chance = jax.random.randint(jax.random.fold_in(rng, 2), (rows, number_of), 0, 4096) + favour
    holders = jax.random.permutation(jax.random.fold_in(rng, 3), rows)[jnp.arange(number_of) % rows]
    chance = jnp.where(jnp.arange(rows)[:, None] == holders[None, :], 1 << 14, chance)
    score = chance * number_of + jnp.arange(number_of)
    return lax.top_k(score.astype(jnp.int32), top)[1].astype(jnp.int32)


def assign_block(own_key, own, number, rows, number_of, top, limit, lean):
    sequence = jax.random.permutation(own_key, number_of)
    heavy_load, common = load_shares(number_of, rows * top, limit, lean, True), load_shares(number_of, rows * top, limit, lean, False)
    places = jnp.arange(number_of)

    def named(tallies, offset_by):
        used = int((tallies > 0).sum())
        fixed = max(1, used // 4)
        passed = fixed + (places - fixed + offset_by * (used - fixed)) % max(1, number_of - fixed)
        return jnp.zeros((number_of,), jnp.int32).at[sequence[jnp.where(places < fixed, places, passed)]].set(jnp.asarray(tallies, jnp.int32))

    tallies = jnp.where(number % 4 == 0, named(heavy_load, number // 4), named(common, number - number // 4 - 1))
    mixed = jax.random.permutation(jax.random.fold_in(own, 3), number_of)
    source_of, receiver = mixed[0:number_of // 2 * 2:2], mixed[1:number_of // 2 * 2:2]
    margin = jnp.minimum(tallies[source_of] - 1, limit - tallies[receiver]) // 2
    margin = jnp.where((source_of == sequence[0]) | (receiver == sequence[0]) | (tallies[receiver] == 0), 0, jnp.maximum(margin, 0))
    passed = jax.random.randint(jax.random.fold_in(own, 4), (number_of // 2,), 0, 1 << 20) % (margin + 1)
    tallies = tallies.at[source_of].add(-passed).at[receiver].add(passed)
    members = jnp.searchsorted(jnp.cumsum(tallies), jnp.arange(rows * top), side="right").astype(jnp.int32)
    listing = members.reshape(top, rows).T
    listing = listing[jax.random.permutation(jax.random.fold_in(own, 1), rows)]
    offset_by = jax.random.randint(jax.random.fold_in(own, 2), (rows, 1), 0, top)
    return jnp.take_along_axis(listing, (jnp.arange(top)[None, :] + offset_by) % top, axis=1)


def load_shares(number_of, total, most, lean, full):
    weights = [(1 << 20) // math.isqrt(rank ** lean) + 1 for rank in range(1, number_of + 1)]
    largest = most if full else min(most, max(-(-total // number_of), total * weights[0] // sum(weights)))
    least = 1 if total - largest >= number_of - 1 else 0
    holding, rest = [largest] + [least] * (number_of - 1), total - largest - least * (number_of - 1)
    while rest > 0:
        free = [i for i in range(1, number_of) if holding[i] < largest] or [i for i in range(1, number_of) if holding[i] < most]
        pool, remaining = sum([weights[i] for i in free]), rest
        for i in free:
            more = min(most - holding[i], max(1, remaining * weights[i] // pool), rest)
            holding[i] = holding[i] + more
            rest = rest - more
    return np.array(holding)


def setup_inputs(seed: int = 0) -> dict:
    key_of = jax.random.split(jax.random.key(seed), 6)
    sph_state = draw_sph_state(jax.random.fold_in(key_of[5], 71), 0)
    sph_dest_keys = jax.random.split(jax.random.fold_in(key_of[1], 1), SPHERES // SPH_DEV)
    sph_dest_turns = jax.random.permutation(jax.random.fold_in(key_of[1], 3), SPHERES // SPH_DEV)
    sph_dest = jax.vmap(lambda own, number: assign_block(jax.random.fold_in(key_of[1], 2), own, number, SPH_DEV, DEVROWS, 1, CAP, 1))(sph_dest_keys, sph_dest_turns).reshape((SPHERES, 1))
    body_list = choose_distinct(key_of[2], DEVROWS, BODIES, OVL, 2048)
    tile_codes = draw_tile_codes(jax.random.fold_in(key_of[5], 71), 0)
    triangles = draw_triangles(jax.random.fold_in(key_of[5], 71), 0)
    return dict(sph_state=sph_state, sph_dest=sph_dest, body_list=body_list, tile_codes=tile_codes, triangles=triangles)


stiff_pair = 50.0
damp_pair = 2.0
stiff_wall = 50.0
time_step = 0.01
gravity = 9.81
body_mass = 4.0
body_inertia = 40.0


def contact(spheres, facets):
    centre = spheres[0:3]
    radius = spheres[3]
    corner = facets[0:3]
    edge_one = facets[3:6] - corner
    edge_two = facets[6:9] - corner
    square_one = jnp.sum(edge_one * edge_one, 0)
    square_two = jnp.sum(edge_two * edge_two, 0)
    cross_term = jnp.sum(edge_one * edge_two, 0)
    inverse = 1.0 / (square_one * square_two - cross_term * cross_term)
    relative = centre[:, :, None] - corner[:, None, :]
    along_one = jnp.sum(relative * edge_one[:, None, :], 0)
    along_two = jnp.sum(relative * edge_two[:, None, :], 0)
    weight_b = (square_two * along_one - cross_term * along_two) * inverse
    weight_c = (square_one * along_two - cross_term * along_one) * inverse
    weight_a = jnp.maximum(1.0 - weight_b - weight_c, 0.0)
    weight_b = jnp.maximum(weight_b, 0.0)
    weight_c = jnp.maximum(weight_c, 0.0)
    totals = weight_a + weight_b + weight_c
    weight_b = weight_b / totals
    weight_c = weight_c / totals
    nearest = corner[:, None, :] + weight_b[None] * edge_one[:, None, :] + weight_c[None] * edge_two[:, None, :]
    offset = centre[:, :, None] - nearest
    squared = jnp.sum(offset * offset, 0)
    strength = stiff_wall * jnp.maximum(radius[:, None] * radius[:, None] - squared, 0.0)
    forces = strength[None] * offset
    on_spheres = jnp.sum(forces, 2)
    on_body = -jnp.sum(forces, (1, 2))
    torque = -jnp.sum(jnp.cross(nearest, forces, axis=0), (1, 2))
    return on_spheres, jnp.concatenate([on_body, torque])


def tile_forces(spheres, facets, tile_list):
    tiles_tri = facets.shape[1] // 128

    def advance_tile(carried, tile_code):
        forces, wrench = carried
        sphere_tile = tile_code // tiles_tri
        facet_tile = tile_code % tiles_tri
        sphere_part = lax.dynamic_slice_in_dim(spheres, sphere_tile * 128, 128, 1)
        facet_part = lax.dynamic_slice_in_dim(facets, facet_tile * 128, 128, 1)
        on_spheres, on_body = contact(sphere_part, facet_part)
        current = lax.dynamic_slice_in_dim(forces, sphere_tile * 128, 128, 1)
        forces = lax.dynamic_update_slice_in_dim(forces, current + on_spheres, sphere_tile * 128, 1)
        return (forces, wrench + on_body), None

    initial = (jnp.zeros((3, spheres.shape[1]), jnp.float32), jnp.zeros((6,), jnp.float32))
    (forces, wrench), unused = lax.scan(advance_tile, initial, tile_list)
    return forces, wrench


def sphere_forces(sphere_block):
    position = sphere_block[0:3]
    velocity = sphere_block[3:6]
    radius = sphere_block[6]
    occupied = (radius > 0).astype(jnp.float32)
    coords = jnp.concatenate([position, radius[None]], 0)
    baseline = radius * radius - jnp.sum(position * position, 0)
    inner_products = lax.dot_general(coords, coords, (((0,), (0,)), ((), ())), precision=lax.Precision.HIGHEST)
    intersection = jnp.maximum(baseline[:, None] + baseline[None, :] + 2.0 * inner_products, 0.0)
    intersection = intersection * occupied[:, None] * occupied[None, :]
    stacked = jnp.concatenate([position, velocity, jnp.ones((1, position.shape[1]), jnp.float32)], 0)
    weighted = lax.dot_general(stacked, intersection, (((1,), (1,)), ((), ())), precision=lax.Precision.HIGHEST)
    totals = weighted[6]
    return stiff_pair * (totals * position - weighted[0:3]) - damp_pair * (totals * velocity - weighted[3:6])


def advance(sphere_block, forces):
    position = sphere_block[0:3]
    velocity = sphere_block[3:6]
    radius = sphere_block[6]
    occupied = radius > 0
    masses = jnp.where(occupied, radius * radius * radius, 1.0)
    falling = jnp.array([0.0, 0.0, gravity], jnp.float32)
    acceleration = forces / masses[None] - falling[:, None]
    velocity_new = velocity + time_step * acceleration
    position_new = position + time_step * velocity_new
    result = jnp.concatenate([position_new, velocity_new, radius[None]], 0)
    return jnp.where(occupied[None], result, 0.0)


def migrate(sph_state, sph_dest):
    ndevices = N_SECTOR * N_BIN
    targets = sph_dest[:, 0].reshape(ndevices, SPH_DEV)

    def ranking(target_row):
        onehot = (target_row[:, None] == jnp.arange(ndevices, dtype=jnp.int32)[None, :]).astype(jnp.int32)
        return jnp.sum((jnp.cumsum(onehot, 0) - 1) * onehot, 1).astype(jnp.int32)

    ranks = lax.map(ranking, targets)
    sources = jnp.arange(ndevices, dtype=jnp.int32)[:, None]
    columns = (targets * (ndevices * CAP) + sources * CAP + ranks).reshape(-1)
    return jnp.zeros((7, SLOTS), jnp.float32).at[:, columns].set(sph_state)


def reference(sph_state, sph_dest, body_list, tile_codes, triangles):
    ndevices = N_SECTOR * N_BIN
    slots = migrate(sph_state, sph_dest)
    blocks = jnp.transpose(slots.reshape(7, ndevices, 2 * SPH_DEV), (1, 0, 2))
    device_ids = jnp.arange(ndevices, dtype=jnp.int32)

    def one_device(operands):
        sphere_block, bodies, tile_rows, device_id = operands
        bin_index = (device_id % N_BIN).astype(jnp.int32)
        forces = sphere_forces(sphere_block)
        coords = jnp.concatenate([sphere_block[0:3], sphere_block[6:7]], 0)
        wall_total = jnp.zeros_like(forces)
        wrench_rows = []
        for slot_index in range(OVL):
            facets = lax.dynamic_slice(triangles, (jnp.int32(0), bodies[slot_index].astype(jnp.int32), bin_index * TBLK), (9, 1, TBLK))[:, 0, :]
            on_spheres, on_body = tile_forces(coords, facets, tile_rows[slot_index])
            wall_total = wall_total + on_spheres
            wrench_rows.append(on_body)
        return advance(sphere_block, forces + wall_total), jnp.stack(wrench_rows)

    new_blocks, wrench_parts = lax.map(one_device, (blocks, body_list, tile_codes, device_ids))
    new_state = jnp.transpose(new_blocks, (1, 0, 2)).reshape(7, SLOTS)
    wrench = jnp.zeros((BODIES, 6), jnp.float32).at[body_list.reshape(-1)].add(wrench_parts.reshape(-1, 6))
    scaling = jnp.array([time_step / body_mass] * 3 + [time_step / body_inertia] * 3, jnp.float32)
    return new_state, wrench * scaling[None, :]
```

```python
import functools

import jax
import jax.numpy as jnp
from jax import lax
from jax.experimental import pallas as pl
from jax.experimental.pallas import tpu as pltpu
from jax.sharding import PartitionSpec as P

stiff_pair = 50.0
damp_pair = 2.0
stiff_wall = 50.0
time_step = 0.01
gravity = 9.81
body_mass = 4.0
body_inertia = 40.0

MESH = pl.DeviceIdType.MESH
N = 16
HOLDERS = 12
f32, bf16, i32 = jnp.float32, jnp.bfloat16, jnp.int32


def split3(value):
    high = value.astype(bf16).astype(f32)
    rest = value - high
    middle = rest.astype(bf16).astype(f32)
    return high, middle, rest - middle


def is_holder(s):
    return (s // 4) != (s % 4)


def piece_of(s):
    y, x = s // 4, s % 4
    return 3 * y + x - jnp.where(x > y, 1, 0)


def holder_at(piece):
    y, x = piece // 3, piece % 3
    return 4 * y + x + (1 if x >= y else 0)


def greet(sector, bin_):
    barrier = pltpu.get_barrier_semaphore()
    for off in range(1, N):
        pl.semaphore_signal(barrier, inc=1, device_id=(sector, lax.rem(bin_ + off, N)), device_id_type=MESH)
        pl.semaphore_signal(barrier, inc=1, device_id=(lax.rem(sector + off, N), bin_), device_id_type=MESH)
    return barrier


def outgoing_tiles(state_ref, dest_ref, out_ref):
    leaving = state_ref.shape[1]
    dest = dest_ref[...]
    width = 256
    row = lax.broadcasted_iota(i32, (256, width), 0)
    before = (row < lax.broadcasted_iota(i32, (256, width), 1)).astype(bf16)
    counting = jnp.concatenate([before, jnp.ones((256, width), bf16)], 1)
    carry = jnp.zeros((256, width), f32)
    ranks = []
    for part in range(leaving // width):
        hit = row == dest[:, part * width : (part + 1) * width]
        counted = jnp.dot(hit.astype(bf16), counting, preferred_element_type=f32)
        ranks.append(jnp.sum(jnp.where(hit, counted[:, :width] + carry, 0.0), 0, keepdims=True))
        carry = carry + counted[:, width:]
    rank = jnp.concatenate(ranks, 1).astype(i32)
    key = (dest // N) * 8 + rank
    picks = (lax.broadcasted_iota(i32, (128, leaving), 0) == key).astype(bf16)
    state = state_ref[...]
    state = jnp.concatenate([state, jnp.zeros((1, leaving), f32)], 0)
    stacked = jnp.concatenate(split3(state), 0)
    lane_bin = dest % N
    chosen = [jnp.where(lane_bin == db, stacked, 0.0) for db in range(N)]
    chosen = jnp.concatenate(chosen, 0).astype(bf16)
    placed = lax.dot_general(chosen, picks, (((1,), (1,)), ((), ())), preferred_element_type=f32)
    for db in range(N):
        base = 24 * db
        out_ref[db] = placed[base : base + 8] + placed[base + 8 : base + 16] + placed[base + 16 : base + 24]


def swap_groups(tiles):
    lane = lax.broadcasted_iota(i32, (8, 128), 1)
    for bit in (1, 2, 4, 8):
        low = (lane // 8) % (2 * bit) < bit
        fresh = list(tiles)
        for a in range(N):
            if a & bit == 0:
                b = a | bit
                fresh[a] = jnp.where(low, tiles[a], pltpu.roll(tiles[b], 8 * bit, 1))
                fresh[b] = jnp.where(low, pltpu.roll(tiles[a], 128 - 8 * bit, 1), tiles[b])
        tiles = fresh
    return tiles


def exchange_kernel(
    state_ref, dest_ref, body_ref, tri_ref, sph_out, sel_out,
    out1, got1, out2, got2, piece, sel_send, sel_got, names, names_got, names_smem,
    s1, r1, s2, r2, t1s, t1r, ns, nr, t2s, t2r, own_sem, names_sem,
):
    sector, bin_ = lax.axis_index("sector"), lax.axis_index("bin")
    barrier = greet(sector, bin_)
    outgoing_tiles(state_ref, dest_ref, out1)
    lane = lax.broadcasted_iota(i32, (1, 128), 1)
    names[...] = jnp.where(lane == 0, body_ref[0, 0], body_ref[0, 1])
    pl.semaphore_wait(barrier, 2 * (N - 1))

    def sphere_one(src, dst):
        return pltpu.make_async_remote_copy(
            src_ref=out1.at[dst], dst_ref=got1.at[src], send_sem=s1.at[dst], recv_sem=r1.at[src],
            device_id=(sector, dst), device_id_type=MESH,
        )

    def sphere_two(src, dst):
        return pltpu.make_async_remote_copy(
            src_ref=out2.at[dst], dst_ref=got2.at[src], send_sem=s2.at[dst], recv_sem=r2.at[src],
            device_id=(dst, bin_), device_id_type=MESH,
        )

    def piece_one(src, dst):
        return pltpu.make_async_remote_copy(
            src_ref=tri_ref.at[pl.ds(3 * piece_of(dst), 3)], dst_ref=piece.at[src], send_sem=t1s.at[dst], recv_sem=t1r.at[src],
            device_id=(dst, bin_), device_id_type=MESH,
        )

    def names_one(src, dst):
        return pltpu.make_async_remote_copy(
            src_ref=names, dst_ref=names_got.at[src], send_sem=ns.at[dst], recv_sem=nr.at[src],
            device_id=(dst, bin_), device_id_type=MESH,
        )

    def piece_two(src, dst):
        return pltpu.make_async_remote_copy(
            src_ref=sel_send.at[dst], dst_ref=sel_got.at[piece_of(src)], send_sem=t2s.at[dst], recv_sem=t2r.at[src],
            device_id=(dst, bin_), device_id_type=MESH,
        )

    def peers(me):
        return [lax.rem(me + off, N) for off in range(1, N)]

    holding = is_holder(sector)
    for peer in peers(bin_):
        sphere_one(bin_, peer).start()
    for peer in peers(sector):

        @pl.when(is_holder(peer))
        def _(peer=peer):
            piece_one(sector, peer).start()
            names_one(sector, peer).start()

    @pl.when(holding)
    def _():
        own = pltpu.make_async_copy(tri_ref.at[pl.ds(3 * piece_of(sector), 3)], piece.at[sector], own_sem)
        own.start()
        names_got[sector] = names[...]
        own.wait()

    got1[bin_] = out1[bin_]
    for peer in peers(bin_):
        sphere_one(peer, bin_).wait_recv()
    for ds, tile in enumerate(swap_groups([got1[sb] for sb in range(N)])):
        out2[ds] = tile
    for peer in peers(sector):
        sphere_two(sector, peer).start()
    got2[sector] = out2[sector]

    @pl.when(holding)
    def _():
        for peer in peers(sector):
            names_one(peer, sector).wait_recv()
        listed = pltpu.make_async_copy(names_got, names_smem, names_sem)
        listed.start()
        for peer in peers(sector):
            piece_one(peer, sector).wait_recv()
        listed.wait()
        for dst in range(N):
            for entry in range(2):
                sel_send[dst, entry] = piece[names_smem[dst, 0, entry]]
        for peer in peers(sector):
            piece_two(sector, peer).start()
        sel_got[piece_of(sector)] = sel_send[sector]

    for peer in peers(sector):
        sphere_two(peer, sector).wait_recv()
    for ss in range(N):
        sph_out[ss] = got2[ss]
    for peer in peers(sector):

        @pl.when(is_holder(peer))
        def _(peer=peer):
            piece_two(peer, sector).wait_recv()

    for p in range(HOLDERS):
        sel_out[p] = sel_got[p]

    for peer in peers(bin_):
        sphere_one(bin_, peer).wait_send()
    for peer in peers(sector):
        sphere_two(sector, peer).wait_send()

        @pl.when(is_holder(peer))
        def _(peer=peer):
            piece_one(sector, peer).wait_send()
            names_one(sector, peer).wait_send()

    @pl.when(holding)
    def _():
        for peer in peers(sector):
            piece_two(sector, peer).wait_send()


def exchange(state, dest, bodies, tri):
    dma = pltpu.SemaphoreType.DMA
    return pl.pallas_call(
        exchange_kernel,
        out_shape=(
            jax.ShapeDtypeStruct((N, 8, 128), f32),
            jax.ShapeDtypeStruct((HOLDERS, 2, 3, 8, 128), f32),
        ),
        in_specs=[
            pl.BlockSpec(memory_space=pltpu.VMEM),
            pl.BlockSpec(memory_space=pltpu.VMEM),
            pl.BlockSpec(memory_space=pltpu.SMEM),
            pl.BlockSpec(memory_space=pl.ANY),
        ],
        out_specs=(pl.BlockSpec(memory_space=pltpu.VMEM), pl.BlockSpec(memory_space=pltpu.VMEM)),
        scratch_shapes=[
            pltpu.VMEM((N, 8, 128), f32),
            pltpu.VMEM((N, 8, 128), f32),
            pltpu.VMEM((N, 8, 128), f32),
            pltpu.VMEM((N, 8, 128), f32),
            pltpu.VMEM((N, 3, 8, 128), f32),
            pltpu.VMEM((N, 2, 3, 8, 128), f32),
            pltpu.VMEM((HOLDERS, 2, 3, 8, 128), f32),
            pltpu.VMEM((1, 128), i32),
            pltpu.VMEM((N, 1, 128), i32),
            pltpu.SMEM((N, 1, 128), i32),
        ]
        + [dma((N,))] * 10
        + [dma, dma],
        compiler_params=pltpu.CompilerParams(
            collective_id=0, has_side_effects=True, vmem_limit_bytes=32 * 2**20
        ),
    )(state, dest, bodies, tri)


def pair_features(sph):
    width = sph.shape[1]
    position, radius = sph[0:3], sph[6:7]
    base = radius * radius - jnp.sum(position * position, 0, keepdims=True)
    base = jnp.where(radius > 0, base, -1e30)
    high, middle, low = split3(jnp.concatenate([position, radius], 0))
    base = jnp.concatenate(split3(base), 0)
    one = jnp.ones((3, width), f32)
    none = jnp.zeros((2, width), f32)
    left = [2.0 * high, 2.0 * high, 2.0 * middle, 2.0 * middle, 2.0 * high, 2.0 * low, base, one, none]
    right = [high, middle, high, middle, low, high, one, base, none]
    row = lax.broadcasted_iota(i32, sph.shape, 0)
    weighed = jnp.where(row == 6, 1.0, sph)
    high, middle, low = split3(weighed)
    stacked = jnp.concatenate([high, middle, low, jnp.zeros_like(high)], 0)
    return (
        jnp.concatenate(left, 0).astype(bf16),
        jnp.concatenate(right, 0).astype(bf16),
        stacked.astype(bf16),
    )


def triangle_features(corner):
    a, e1, e2 = corner[0:3], [corner[3 + k] - corner[k] for k in range(3)], [corner[6 + k] - corner[k] for k in range(3)]
    d11 = e1[0] * e1[0] + e1[1] * e1[1] + e1[2] * e1[2]
    d12 = e1[0] * e2[0] + e1[1] * e2[1] + e1[2] * e2[2]
    d22 = e2[0] * e2[0] + e2[1] * e2[1] + e2[2] * e2[2]
    inverse = 1.0 / (d11 * d22 - d12 * d12)
    for_b = [(d22 * e1[k] - d12 * e2[k]) * inverse for k in range(3)]
    for_c = [(d11 * e2[k] - d12 * e1[k]) * inverse for k in range(3)]
    return [*a, *e1, *e2, *for_b, *for_c]


def contact_kernel(
    code_ref, body_ref, sph_ref, sel_ref, state_out, part_out,
    wide, feat, acc, left_ref, stacked_ref, summed,
):
    tiles = sph_ref.shape[0]
    entries = code_ref.shape[0]
    sph = jnp.concatenate([sph_ref[t] for t in range(tiles)], 1)

    left, right, stacked = pair_features(sph)
    left_ref[...] = left
    stacked_ref[...] = stacked
    summed[...] = jnp.zeros_like(summed)
    rows = 256

    def row_group(step, carry):
        start = pl.multiple_of(step * rows, rows)
        gap = lax.dot_general(
            left_ref[:, pl.ds(start, rows)], right, (((0,), (0,)), ((), ())), preferred_element_type=f32
        )
        inter = jnp.maximum(gap, 0.0)
        high = inter.astype(bf16)
        low = (inter - high.astype(f32)).astype(bf16)
        weighed = stacked_ref[:, pl.ds(start, rows)]
        summed[...] += jnp.dot(weighed, high, preferred_element_type=f32) + jnp.dot(
            weighed, low, preferred_element_type=f32
        )
        return carry

    lax.fori_loop(0, tiles * 128 // rows, row_group, 0)

    for entry in range(entries):
        for group in range(4):
            corner = []
            for c in range(9):
                at = c * 4 + group
                corner.append(sel_ref[at // 3, entry, at % 3])
            for f, value in enumerate(triangle_features(corner)):
                feat[entry, f, pl.ds(8 * group, 8), :] = value
    for t in range(tiles):
        turned = sph_ref[t].T
        for f, c in enumerate((0, 1, 2, 6)):
            column = turned[:, c : c + 1]
            if c == 6:
                column = column * column
            wide[f, pl.ds(128 * t, 128), :] = jnp.broadcast_to(column, (128, 128))
    acc[...] = jnp.zeros_like(acc)
    for entry in range(entries):

        def tile_pair(step, carry, entry=entry):
            code = code_ref[entry, step]
            st, tt = code // 32, code % 32
            ax, ay, az, ux, uy, uz, wx, wy, wz, bx, by, bz, cx, cy, cz = (
                jnp.broadcast_to(feat[entry, f, pl.ds(tt, 1), :], (8, 128)) for f in range(15)
            )
            for group in range(16):
                at = pl.ds(pl.multiple_of(st * 128 + 8 * group, 8), 8)
                dx, dy, dz = wide[0, at, :] - ax, wide[1, at, :] - ay, wide[2, at, :] - az
                b = bx * dx + by * dy + bz * dz
                c = cx * dx + cy * dy + cz * dz
                a = jnp.maximum((1.0 - b) - c, 0.0)
                b = jnp.maximum(b, 0.0)
                c = jnp.maximum(c, 0.0)
                total = a + b + c
                inverse = pl.reciprocal(total, approx=True)
                inverse = inverse * (2.0 - total * inverse)
                b, c = b * inverse, c * inverse
                ox = dx - b * ux - c * wx
                oy = dy - b * uy - c * wy
                oz = dz - b * uz - c * wz
                strength = jnp.maximum(wide[3, at, :] - (ox * ox + oy * oy + oz * oz), 0.0)
                here = pl.ds(8 * group, 8)
                acc[entry, st, 0, here, :] += strength * ox
                acc[entry, st, 1, here, :] += strength * oy
                acc[entry, st, 2, here, :] += strength * oz
            return carry

        lax.fori_loop(0, code_ref.shape[1], tile_pair, 0)

    summed_all = summed[...]
    weighted = summed_all[0:8] + summed_all[8:16] + summed_all[16:24]
    ones = jnp.ones((16, 128), bf16)
    wrench = [[jnp.zeros((1, 128), f32)] * 6 for _ in range(entries)]
    for t in range(tiles):
        lanes = slice(128 * t, 128 * t + 128)
        tile = sph_ref[t]
        pos, vel, radius = [tile[k : k + 1] for k in range(3)], [tile[3 + k : 4 + k] for k in range(3)], tile[6:7]
        wall = [jnp.zeros((1, 128), f32)] * 3
        for entry in range(entries):
            force = []
            for k in range(3):
                block = acc[entry, t, k]
                high = block.astype(bf16)
                low = (block - high.astype(f32)).astype(bf16)
                dims = (((1,), (1,)), ((), ()))
                total = lax.dot_general(ones, high, dims, preferred_element_type=f32) + lax.dot_general(
                    ones, low, dims, preferred_element_type=f32
                )
                force.append(stiff_wall * total[0:1])
            wall = [wall[k] + force[k] for k in range(3)]
            moment = [
                pos[1] * force[2] - pos[2] * force[1],
                pos[2] * force[0] - pos[0] * force[2],
                pos[0] * force[1] - pos[1] * force[0],
            ]
            wrench[entry] = [w - f for w, f in zip(wrench[entry], force + moment)]
        live = radius > 0
        mass = jnp.where(live, radius * radius * radius, 1.0)
        totals = weighted[6:7, lanes]
        out_pos, out_vel = [], []
        for k in range(3):
            pair = stiff_pair * (totals * pos[k] - weighted[k : k + 1, lanes]) - damp_pair * (
                totals * vel[k] - weighted[3 + k : 4 + k, lanes]
            )
            acceleration = (pair + wall[k]) / mass - (gravity if k == 2 else 0.0)
            fresh = vel[k] + time_step * acceleration
            out_vel.append(fresh)
            out_pos.append(pos[k] + time_step * fresh)
        block = jnp.concatenate([*out_pos, *out_vel, radius], 0)
        state_out[:, lanes] = jnp.where(live, block, 0.0)

    lane = lax.broadcasted_iota(i32, (1, 128), 1)
    row = lax.broadcasted_iota(i32, (N, 1, 128), 0)
    part = jnp.zeros((N, 1, 128), f32)
    for entry in range(entries):
        line = jnp.zeros((1, 128), f32)
        for k in range(6):
            line = jnp.where(lane == k, jnp.sum(wrench[entry][k], 1, keepdims=True), line)
        part = part + jnp.where(row == body_ref[0, entry], line[None], 0.0)
    part_out[...] = part


def contacts(codes, bodies, sph, sel):
    slots = sph.shape[0] * 128
    smem, vmem = pl.BlockSpec(memory_space=pltpu.SMEM), pl.BlockSpec(memory_space=pltpu.VMEM)
    return pl.pallas_call(
        contact_kernel,
        out_shape=(jax.ShapeDtypeStruct((7, slots), f32), jax.ShapeDtypeStruct((N, 1, 128), f32)),
        in_specs=[smem, smem, vmem, vmem],
        out_specs=(vmem, vmem),
        scratch_shapes=[
            pltpu.VMEM((4, slots, 128), f32),
            pltpu.VMEM((2, 15, 32, 128), f32),
            pltpu.VMEM((2, sph.shape[0], 3, 128, 128), f32),
            pltpu.VMEM((32, slots), bf16),
            pltpu.VMEM((32, slots), bf16),
            pltpu.VMEM((32, slots), f32),
        ],
        compiler_params=pltpu.CompilerParams(vmem_limit_bytes=48 * 2**20),
    )(codes, bodies, sph, sel)


def wrench_kernel(part_ref, out_ref, sent, got1, row, got2, s1, r1, s2, r2):
    sector, bin_ = lax.axis_index("sector"), lax.axis_index("bin")
    barrier = greet(sector, bin_)
    for k in range(N):
        sent[k] = part_ref[k]
    pl.semaphore_wait(barrier, 2 * (N - 1))

    def one(src, dst):
        return pltpu.make_async_remote_copy(
            src_ref=sent.at[dst], dst_ref=got1.at[src], send_sem=s1.at[dst], recv_sem=r1.at[src],
            device_id=(dst, bin_), device_id_type=MESH,
        )

    def two(src, dst):
        return pltpu.make_async_remote_copy(
            src_ref=row, dst_ref=got2.at[src], send_sem=s2.at[dst], recv_sem=r2.at[src],
            device_id=(sector, dst), device_id_type=MESH,
        )

    def peers(me):
        return [lax.rem(me + off, N) for off in range(1, N)]

    for peer in peers(sector):
        one(sector, peer).start()
    got1[sector] = sent[sector]
    for peer in peers(sector):
        one(peer, sector).wait_recv()
    row[...] = functools.reduce(jnp.add, [got1[k] for k in range(N)])
    for peer in peers(bin_):
        two(bin_, peer).start()
    got2[bin_] = row[...]
    for peer in peers(bin_):
        two(peer, bin_).wait_recv()
    total = functools.reduce(jnp.add, [got2[k] for k in range(N)])
    lane = lax.broadcasted_iota(i32, (1, 128), 1)
    total = total * jnp.where(lane < 3, time_step / body_mass, time_step / body_inertia)
    out_ref[...] = total[:, 0:6]
    for peer in peers(sector):
        one(sector, peer).wait_send()
    for peer in peers(bin_):
        two(bin_, peer).wait_send()


def wrench_sum(part):
    dma = pltpu.SemaphoreType.DMA
    line = pltpu.VMEM((N, 1, 128), f32)
    return pl.pallas_call(
        wrench_kernel,
        out_shape=jax.ShapeDtypeStruct((1, 6), f32),
        in_specs=[pl.BlockSpec(memory_space=pltpu.VMEM)],
        out_specs=pl.BlockSpec(memory_space=pltpu.VMEM),
        scratch_shapes=[line, line, pltpu.VMEM((1, 128), f32), line] + [dma((N,))] * 4,
        compiler_params=pltpu.CompilerParams(collective_id=1, has_side_effects=True),
    )(part)


def local(sph_state, sph_dest, body_list, tile_codes, triangles):
    dest = sph_dest.reshape(1, -1)
    tri = triangles.reshape(36, 8, 128)
    sph, sel = exchange(sph_state, dest, body_list, tri)
    new_block, part = contacts(tile_codes[0], body_list, sph, sel)
    return new_block, wrench_sum(part)


def solution(mesh):
    return jax.shard_map(
        local,
        mesh=mesh,
        in_specs=(
            P(None, ("sector", "bin")),
            P(("sector", "bin"), None),
            P(("sector", "bin"), None),
            P(("sector", "bin"), None, None),
            P(None, "sector", "bin"),
        ),
        out_specs=(P(None, ("sector", "bin")), P("sector", None)),
        check_vma=False,
    )
```

```python
import functools

import jax
import jax.numpy as jnp
from jax import lax
from jax.experimental import pallas as pl
from jax.experimental.pallas import tpu as pltpu
from jax.sharding import PartitionSpec as P

stiff_pair = 50.0
damp_pair = 2.0
stiff_wall = 50.0
time_step = 0.01
gravity = 9.81
body_mass = 4.0
body_inertia = 40.0

MESH = pl.DeviceIdType.MESH
N = 16
HOLDERS = 12
f32, bf16, i32 = jnp.float32, jnp.bfloat16, jnp.int32


def split3(value):
    high = value.astype(bf16).astype(f32)
    rest = value - high
    middle = rest.astype(bf16).astype(f32)
    return high, middle, rest - middle


def is_holder(s):
    return (s // 4) != (s % 4)


def piece_of(s):
    y, x = s // 4, s % 4
    return 3 * y + x - jnp.where(x > y, 1, 0)


def holder_at(piece):
    y, x = piece // 3, piece % 3
    return 4 * y + x + (1 if x >= y else 0)


def greet(sector, bin_):
    barrier = pltpu.get_barrier_semaphore()
    for off in range(1, N):
        pl.semaphore_signal(barrier, inc=1, device_id=(sector, lax.rem(bin_ + off, N)), device_id_type=MESH)
        pl.semaphore_signal(barrier, inc=1, device_id=(lax.rem(sector + off, N), bin_), device_id_type=MESH)
    return barrier


def outgoing_tiles(state_ref, dest_ref, out_ref):
    leaving = state_ref.shape[1]
    dest = dest_ref[...]
    width = 256
    row = lax.broadcasted_iota(i32, (256, width), 0)
    before = (row < lax.broadcasted_iota(i32, (256, width), 1)).astype(bf16)
    counting = jnp.concatenate([before, jnp.ones((256, width), bf16)], 1)
    carry = jnp.zeros((256, width), f32)
    ranks = []
    for part in range(leaving // width):
        hit = row == dest[:, part * width : (part + 1) * width]
        counted = jnp.dot(hit.astype(bf16), counting, preferred_element_type=f32)
        ranks.append(jnp.sum(jnp.where(hit, counted[:, :width] + carry, 0.0), 0, keepdims=True))
        carry = carry + counted[:, width:]
    rank = jnp.concatenate(ranks, 1).astype(i32)
    key = (dest // N) * 8 + rank
    picks = (lax.broadcasted_iota(i32, (128, leaving), 0) == key).astype(bf16)
    state = state_ref[...]
    state = jnp.concatenate([state, jnp.zeros((1, leaving), f32)], 0)
    stacked = jnp.concatenate(split3(state), 0)
    lane_bin = dest % N
    chosen = [jnp.where(lane_bin == db, stacked, 0.0) for db in range(N)]
    chosen = jnp.concatenate(chosen, 0).astype(bf16)
    placed = lax.dot_general(chosen, picks, (((1,), (1,)), ((), ())), preferred_element_type=f32)
    for db in range(N):
        base = 24 * db
        out_ref[db] = placed[base : base + 8] + placed[base + 8 : base + 16] + placed[base + 16 : base + 24]


def swap_groups(tiles):
    lane = lax.broadcasted_iota(i32, (8, 128), 1)
    for bit in (1, 2, 4, 8):
        low = (lane // 8) % (2 * bit) < bit
        fresh = list(tiles)
        for a in range(N):
            if a & bit == 0:
                b = a | bit
                fresh[a] = jnp.where(low, tiles[a], pltpu.roll(tiles[b], 8 * bit, 1))
                fresh[b] = jnp.where(low, pltpu.roll(tiles[a], 128 - 8 * bit, 1), tiles[b])
        tiles = fresh
    return tiles


def pair_features(sph):
    width = sph.shape[1]
    position, radius = sph[0:3], sph[6:7]
    base = radius * radius - jnp.sum(position * position, 0, keepdims=True)
    base = jnp.where(radius > 0, base, -1e30)
    high, middle, low = split3(jnp.concatenate([position, radius], 0))
    base = jnp.concatenate(split3(base), 0)
    one = jnp.ones((3, width), f32)
    none = jnp.zeros((2, width), f32)
    left = [2.0 * high, 2.0 * high, 2.0 * middle, 2.0 * middle, 2.0 * high, 2.0 * low, base, one, none]
    right = [high, middle, high, middle, low, high, one, base, none]
    row = lax.broadcasted_iota(i32, sph.shape, 0)
    weighed = jnp.where(row == 6, 1.0, sph)
    high, middle, low = split3(weighed)
    stacked = jnp.concatenate([high, middle, low, jnp.zeros_like(high)], 0)
    return (
        jnp.concatenate(left, 0),
        jnp.concatenate(right, 0).astype(bf16),
        stacked.astype(bf16),
    )


def triangle_features(corner):
    a, e1, e2 = corner[0:3], [corner[3 + k] - corner[k] for k in range(3)], [corner[6 + k] - corner[k] for k in range(3)]
    d11 = e1[0] * e1[0] + e1[1] * e1[1] + e1[2] * e1[2]
    d12 = e1[0] * e2[0] + e1[1] * e2[1] + e1[2] * e2[2]
    d22 = e2[0] * e2[0] + e2[1] * e2[1] + e2[2] * e2[2]
    inverse = 1.0 / (d11 * d22 - d12 * d12)
    for_b = [(d22 * e1[k] - d12 * e2[k]) * inverse for k in range(3)]
    for_c = [(d11 * e2[k] - d12 * e1[k]) * inverse for k in range(3)]
    for g in (for_b, for_c):
        g.append(-(g[0] * a[0] + g[1] * a[1] + g[2] * a[2]))
    return [*a, *e1, *e2], [for_b, for_c]


def set_triangles(sel_ref, plain_ref, linear_ref):
    for entry in range(2):
        for group in range(4):
            corner = []
            for c in range(9):
                at = c * 4 + group
                corner.append(sel_ref[at // 3, entry, at % 3])
            plain, (for_b, for_c) = triangle_features(corner)
            for f, value in enumerate(plain):
                plain_ref[entry, pl.ds(8 * group, 8), f, :] = value
            for k, value in enumerate(for_b + for_c):
                linear_ref[entry, pl.ds(8 * group, 8), k, :] = value


def set_spheres(sph_ref, wide_ref, point_ref):
    one, none = jnp.ones((1, 128), f32), jnp.zeros((1, 128), f32)
    for t in range(sph_ref.shape[0]):
        tile = sph_ref[t]
        high, middle, low = split3(tile[0:3])
        high, middle, low = [high, one, high, one], [middle, none, middle, none], [low, none, low, none]
        rows = jnp.concatenate([*high, *high, *middle, *middle, *high, *low], 0)
        point_ref[t] = rows.T.astype(bf16)
        turned = tile.T
        for f, c in enumerate((0, 1, 2, 6)):
            column = turned[:, c : c + 1]
            if c == 6:
                column = column * column
            wide_ref[t, f] = jnp.broadcast_to(column, (128, 128))


def wall_tiles(code_ref, entry, plain_ref, linear_ref, wide_ref, point_ref, coef_refs, push_refs, sums_ref, adds_ref):
    count = code_ref.shape[1]
    lane = lax.broadcasted_iota(i32, (128, 128), 1)
    upper = lax.broadcasted_iota(i32, (8, 128), 0) < 4

    def tiles_of(n):
        code = code_ref[entry, n]
        return code >> 5, code & 31

    def weigh(n, coef_ref):
        st, tt = tiles_of(n)
        high, middle, low = split3(linear_ref[entry, tt])
        rows = [high, middle, high, middle, low, high]
        for_b = jnp.concatenate([jnp.where(upper, g, 0.0) for g in rows], 0)
        for_c = jnp.concatenate([jnp.where(upper, 0.0, g) for g in rows], 0)
        coefficients = jnp.concatenate([for_b, for_c], 1).astype(bf16)
        points = point_ref[st]
        coef_ref[...] = jnp.dot(points, coefficients, preferred_element_type=f32)

    def push(n, coef_ref, push_ref):
        st, tt = tiles_of(n)
        ax, ay, az, ux, uy, uz, wx, wy, wz = (
            jnp.broadcast_to(plain_ref[entry, tt, f : f + 1, :], (8, 128)) for f in range(9)
        )

        def eight(group):
            here = slice(8 * group, 8 * group + 8)
            b, c = coef_ref[here, 0:128], coef_ref[here, 128:256]
            a = jnp.maximum((1.0 - b) - c, 0.0)
            b = jnp.maximum(b, 0.0)
            c = jnp.maximum(c, 0.0)
            total = a + b + c
            inverse = pl.reciprocal(total, approx=True)
            inverse = inverse * (2.0 - total * inverse)
            b, c = b * inverse, c * inverse
            ox = (wide_ref[st, 0, here, :] - ax) - b * ux - c * wx
            oy = (wide_ref[st, 1, here, :] - ay) - b * uy - c * wy
            oz = (wide_ref[st, 2, here, :] - az) - b * uz - c * wz
            strength = jnp.maximum(wide_ref[st, 3, here, :] - (ox * ox + oy * oy + oz * oz), 0.0)
            return strength * ox, strength * oy, strength * oz

        for group in range(8):
            here = slice(16 * group, 16 * group + 16)
            for k, both in enumerate(zip(eight(2 * group), eight(2 * group + 1))):
                value = jnp.concatenate(both, 0)
                high = value.astype(bf16)
                push_ref[here, 128 * k : 128 * k + 128] = high
                push_ref[here, 384 + 128 * k : 512 + 128 * k] = (value - high.astype(f32)).astype(bf16)

    def add_up(n, push_ref):
        added = jnp.dot(push_ref[...], adds_ref[...], preferred_element_type=f32)
        sums_ref[entry] = jnp.where((lane & 31) == n, added, sums_ref[entry])

    weigh(0, coef_refs[0])
    push_refs[1][...] = jnp.zeros_like(push_refs[1])

    def two_tiles(i, carry):
        n = 2 * i
        weigh(n + 1, coef_refs[1])
        push(n, coef_refs[0], push_refs[0])
        add_up(n - 1, push_refs[1])
        weigh(jnp.minimum(n + 2, count - 1), coef_refs[0])
        push(n + 1, coef_refs[1], push_refs[1])
        add_up(n, push_refs[0])
        return carry

    lax.fori_loop(0, count // 2, two_tiles, 0)
    add_up(count - 1, push_refs[1])


def set_adds(adds_ref):
    block = lax.broadcasted_iota(i32, (6 * 128, 128), 0) >> 7
    block = jnp.where(block < 3, block, block - 3)
    adds_ref[...] = (block == (lax.broadcasted_iota(i32, (6 * 128, 128), 1) >> 5)).astype(bf16)


def set_pairs(sph_ref, left_ref, right_ref, stacked_ref, summed_ref):
    for t in range(sph_ref.shape[0]):
        left, right, stacked = pair_features(sph_ref[t])
        lanes = slice(128 * t, 128 * t + 128)
        left_ref[pl.ds(128 * t, 128), :] = left.T.astype(bf16)
        right_ref[:, lanes], stacked_ref[:, lanes] = right, stacked
    summed_ref[...] = jnp.zeros_like(summed_ref)


def pair_sums(first, last, left_ref, right_ref, stacked_ref, summed_ref):
    rows = 256

    def row_group(step, carry):
        start = pl.multiple_of(step * rows, rows)
        left = left_ref[pl.ds(start, rows), :]
        weighed = stacked_ref[:, pl.ds(start, rows)]
        for column in range(0, right_ref.shape[1], 256):
            here = slice(column, column + 256)
            gap = jnp.dot(left, right_ref[:, here], preferred_element_type=f32)
            inter = jnp.maximum(gap, 0.0)
            high = inter.astype(bf16)
            low = (inter - high.astype(f32)).astype(bf16)
            summed_ref[:, here] += jnp.dot(weighed, high, preferred_element_type=f32) + jnp.dot(
                weighed, low, preferred_element_type=f32
            )
        return carry

    lax.fori_loop(first, last, row_group, 0)


def wall_forces(codes, entry, sums_ref):
    turned = sums_ref[entry].T
    tiles = lax.broadcasted_iota(i32, (16, codes.shape[1]), 0)
    chosen = (tiles == codes >> 5).astype(f32)
    return [
        stiff_wall * jnp.dot(chosen, turned[32 * k : 32 * k + 32], precision=lax.Precision.HIGHEST, preferred_element_type=f32)
        for k in range(3)
    ]


def wrench_line(sph_ref, force):
    tiles = sph_ref.shape[0]
    pos = [jnp.concatenate([sph_ref[t, k : k + 1, :] for t in range(tiles)], 0) for k in range(3)]
    moment = [
        pos[1] * force[2] - pos[2] * force[1],
        pos[2] * force[0] - pos[0] * force[2],
        pos[0] * force[1] - pos[1] * force[0],
    ]
    lane = lax.broadcasted_iota(i32, (1, 128), 1)
    line = jnp.zeros((1, 128), f32)
    for k, value in enumerate(force + moment):
        line = jnp.where(lane == k, -jnp.sum(jnp.sum(value, 0, keepdims=True), 1, keepdims=True), line)
    return line


def set_state(sph_ref, summed_ref, wall, state_out):
    falling = jnp.where(lax.broadcasted_iota(i32, (3, 128), 0) == 2, gravity, 0.0)
    for t in range(sph_ref.shape[0]):
        lanes = slice(128 * t, 128 * t + 128)
        tile = sph_ref[t]
        pos, vel, radius = tile[0:3], tile[3:6], tile[6:7]
        weighted = summed_ref[0:8, lanes] + summed_ref[8:16, lanes] + summed_ref[16:24, lanes]
        totals = weighted[6:7]
        live = radius > 0
        mass = jnp.where(live, radius * radius * radius, 1.0)
        pair = stiff_pair * (totals * pos - weighted[0:3]) - damp_pair * (totals * vel - weighted[3:6])
        push = jnp.concatenate([wall[k][t : t + 1] for k in range(3)], 0)
        fresh = vel + time_step * ((pair + push) / mass - falling)
        block = jnp.concatenate([pos + time_step * fresh, fresh, radius], 0)
        state_out[:, lanes] = jnp.where(live, block, 0.0)


def step_kernel(
    state_ref, dest_ref, body_ref, code_ref, codes_ref, tri_ref, state_out, kick_out,
    out1, got1, out2, sph, piece, sel_send, sel, names, names_got, names_smem,
    wide, point, plain, linear, coef0, coef1, push0, push1, sums, adds, left, right, stacked, summed,
    part, part_got, row, row_got,
    s1, r1, s2, r2, t1s, t1r, ns, nr, t2s, t2r, w1s, w1r, w2s, w2r, own_sem, names_sem,
):
    sector, bin_ = lax.axis_index("sector"), lax.axis_index("bin")
    barrier = greet(sector, bin_)
    outgoing_tiles(state_ref, dest_ref, out1)
    lane = lax.broadcasted_iota(i32, (1, 128), 1)
    names[...] = jnp.where(lane == 0, body_ref[0, 0], body_ref[0, 1])
    set_adds(adds)
    pl.semaphore_wait(barrier, 2 * (N - 1))

    def along_sector(source, landing, sent, arrived):
        def copy(src, dst):
            return pltpu.make_async_remote_copy(
                src_ref=source(dst), dst_ref=landing(src), send_sem=sent.at[dst], recv_sem=arrived.at[src],
                device_id=(dst, bin_), device_id_type=MESH,
            )

        return copy

    def along_bin(source, landing, sent, arrived):
        def copy(src, dst):
            return pltpu.make_async_remote_copy(
                src_ref=source(dst), dst_ref=landing(src), send_sem=sent.at[dst], recv_sem=arrived.at[src],
                device_id=(sector, dst), device_id_type=MESH,
            )

        return copy

    def peers(me):
        return [lax.rem(me + off, N) for off in range(1, N)]

    sphere_one = along_bin(lambda d: out1.at[d], lambda s: got1.at[s], s1, r1)
    sphere_two = along_sector(lambda d: out2.at[d], lambda s: sph.at[s], s2, r2)
    piece_one = along_sector(lambda d: tri_ref.at[pl.ds(3 * piece_of(d), 3)], lambda s: piece.at[s], t1s, t1r)
    names_one = along_sector(lambda d: names, lambda s: names_got.at[s], ns, nr)
    piece_two = along_sector(lambda d: sel_send.at[d], lambda s: sel.at[piece_of(s)], t2s, t2r)
    wrench_one = along_sector(lambda d: part.at[d], lambda s: part_got.at[s], w1s, w1r)
    wrench_two = along_bin(lambda d: row, lambda s: row_got.at[s], w2s, w2r)

    holding = is_holder(sector)
    for peer in peers(bin_):
        sphere_one(bin_, peer).start()
    for peer in peers(sector):

        @pl.when(is_holder(peer))
        def _(peer=peer):
            names_one(sector, peer).start()
            piece_one(sector, peer).start()

    @pl.when(holding)
    def _():
        own = pltpu.make_async_copy(tri_ref.at[pl.ds(3 * piece_of(sector), 3)], piece.at[sector], own_sem)
        own.start()
        names_got[sector] = names[...]
        own.wait()

    got1[bin_] = out1[bin_]
    for peer in peers(bin_):
        sphere_one(peer, bin_).wait_recv()
    for ds, tile in enumerate(swap_groups([got1[sb] for sb in range(N)])):
        out2[ds] = tile
    for peer in peers(sector):
        sphere_two(sector, peer).start()
    sph[sector] = out2[sector]

    @pl.when(holding)
    def _():
        for peer in peers(sector):
            names_one(peer, sector).wait_recv()
        listed = pltpu.make_async_copy(names_got, names_smem, names_sem)
        listed.start()
        for peer in peers(sector):
            piece_one(peer, sector).wait_recv()
        listed.wait()
        for dst in range(N):
            for entry in range(2):
                sel_send[dst, entry] = piece[names_smem[dst, 0, entry]]
        for peer in peers(sector):
            piece_two(sector, peer).start()
        sel[piece_of(sector)] = sel_send[sector]

    for peer in peers(sector):
        sphere_two(peer, sector).wait_recv()
    set_spheres(sph, wide, point)
    set_pairs(sph, left, right, stacked, summed)
    pair_sums(0, PAIRS_ONE, left, right, stacked, summed)

    for peer in peers(sector):

        @pl.when(is_holder(peer))
        def _(peer=peer):
            piece_two(peer, sector).wait_recv()

    set_triangles(sel, plain, linear)
    body_row = lax.broadcasted_iota(i32, (N, 1, 128), 0)
    parts = jnp.zeros((N, 1, 128), f32)
    wall = [jnp.zeros((16, 128), f32)] * 3
    for entry in range(2):
        sums[entry] = jnp.zeros((128, 128), f32)
        wall_tiles(code_ref, entry, plain, linear, wide, point, (coef0, coef1), (push0, push1), sums, adds)
        force = wall_forces(codes_ref[entry : entry + 1, :], entry, sums)
        wall = [w + g for w, g in zip(wall, force)]
        parts = parts + jnp.where(body_row == body_ref[0, entry], wrench_line(sph, force)[None], 0.0)
    part[...] = parts

    for peer in peers(sector):
        wrench_one(sector, peer).start()
    part_got[sector] = part[sector]
    pair_sums(PAIRS_ONE, PAIRS_TWO, left, right, stacked, summed)
    for peer in peers(sector):
        wrench_one(peer, sector).wait_recv()
    row[...] = functools.reduce(jnp.add, [part_got[k] for k in range(N)])
    for peer in peers(bin_):
        wrench_two(bin_, peer).start()
    row_got[bin_] = row[...]
    pair_sums(PAIRS_TWO, PAIRS_ALL, left, right, stacked, summed)
    set_state(sph, summed, wall, state_out)
    for peer in peers(bin_):
        wrench_two(peer, bin_).wait_recv()
    total = functools.reduce(jnp.add, [row_got[k] for k in range(N)])
    total = total * jnp.where(lane < 3, time_step / body_mass, time_step / body_inertia)
    kick_out[...] = total[:, 0:6]

    for peer in peers(bin_):
        sphere_one(bin_, peer).wait_send()
        wrench_two(bin_, peer).wait_send()
    for peer in peers(sector):
        sphere_two(sector, peer).wait_send()
        wrench_one(sector, peer).wait_send()

        @pl.when(is_holder(peer))
        def _(peer=peer):
            names_one(sector, peer).wait_send()
            piece_one(sector, peer).wait_send()

    @pl.when(holding)
    def _():
        for peer in peers(sector):
            piece_two(sector, peer).wait_send()


PAIRS_ONE, PAIRS_TWO, PAIRS_ALL = 3, 6, 8


def step(state, dest, bodies, codes, tri):
    slots = 2 * state.shape[1]
    smem, vmem = pl.BlockSpec(memory_space=pltpu.SMEM), pl.BlockSpec(memory_space=pltpu.VMEM)
    dma = pltpu.SemaphoreType.DMA
    line = pltpu.VMEM((N, 1, 128), f32)
    tiles = pltpu.VMEM((N, 8, 128), f32)
    return pl.pallas_call(
        step_kernel,
        out_shape=(jax.ShapeDtypeStruct((7, slots), f32), jax.ShapeDtypeStruct((1, 6), f32)),
        in_specs=[vmem, vmem, smem, smem, vmem, pl.BlockSpec(memory_space=pl.ANY)],
        out_specs=(vmem, vmem),
        scratch_shapes=[
            *[tiles] * 4,
            pltpu.VMEM((N, 3, 8, 128), f32),
            pltpu.VMEM((N, 2, 3, 8, 128), f32),
            pltpu.VMEM((HOLDERS, 2, 3, 8, 128), f32),
            pltpu.VMEM((1, 128), i32),
            pltpu.VMEM((N, 1, 128), i32),
            pltpu.SMEM((N, 1, 128), i32),
            pltpu.VMEM((N, 4, 128, 128), f32),
            pltpu.VMEM((N, 128, 48), bf16),
            pltpu.VMEM((2, 32, 16, 128), f32),
            pltpu.VMEM((2, 32, 8, 128), f32),
            pltpu.VMEM((128, 256), f32),
            pltpu.VMEM((128, 256), f32),
            pltpu.VMEM((128, 768), bf16),
            pltpu.VMEM((128, 768), bf16),
            pltpu.VMEM((2, 128, 128), f32),
            pltpu.VMEM((768, 128), bf16),
            pltpu.VMEM((slots, 32), bf16),
            pltpu.VMEM((32, slots), bf16),
            pltpu.VMEM((32, slots), bf16),
            pltpu.VMEM((32, slots), f32),
            line,
            line,
            pltpu.VMEM((1, 128), f32),
            line,
        ]
        + [dma((N,))] * 14
        + [dma, dma],
        compiler_params=pltpu.CompilerParams(collective_id=0, has_side_effects=True, vmem_limit_bytes=40 * 2**20),
    )(state, dest, bodies, codes, codes, tri)


def local(sph_state, sph_dest, body_list, tile_codes, triangles):
    dest = sph_dest.reshape(1, -1)
    tri = triangles.reshape(36, 8, 128)
    return step(sph_state, dest, body_list, tile_codes[0], tri)


def solution(mesh):
    return jax.shard_map(
        local,
        mesh=mesh,
        in_specs=(
            P(None, ("sector", "bin")),
            P(("sector", "bin"), None),
            P(("sector", "bin"), None),
            P(("sector", "bin"), None, None),
            P(None, "sector", "bin"),
        ),
        out_specs=(P(None, ("sector", "bin")), P("sector", None)),
        check_vma=False,
    )
```

```python
import functools

import jax
import jax.numpy as jnp
from jax import lax
from jax.experimental import pallas as pl
from jax.experimental.pallas import tpu as pltpu
from jax.sharding import PartitionSpec as P

stiff_pair = 50.0
damp_pair = 2.0
stiff_wall = 50.0
time_step = 0.01
gravity = 9.81
body_mass = 4.0
body_inertia = 40.0

MESH = pl.DeviceIdType.MESH
N = 16
HOLDERS = 12
f32, bf16, i32 = jnp.float32, jnp.bfloat16, jnp.int32


def split3(value):
    high = value.astype(bf16).astype(f32)
    rest = value - high
    middle = rest.astype(bf16).astype(f32)
    return high, middle, rest - middle


def is_holder(s):
    return (s // 4) != (s % 4)


def piece_of(s):
    y, x = s // 4, s % 4
    return 3 * y + x - jnp.where(x > y, 1, 0)


def holder_at(piece):
    y, x = piece // 3, piece % 3
    return 4 * y + x + (1 if x >= y else 0)


def greet(sector, bin_):
    barrier = pltpu.get_barrier_semaphore()
    for off in range(1, N):
        pl.semaphore_signal(barrier, inc=1, device_id=(sector, lax.rem(bin_ + off, N)), device_id_type=MESH)
        pl.semaphore_signal(barrier, inc=1, device_id=(lax.rem(sector + off, N), bin_), device_id_type=MESH)
    return barrier


def outgoing_tiles(state_ref, dest_ref, out_ref):
    leaving = state_ref.shape[1]
    dest = dest_ref[...]
    width = 256
    row = lax.broadcasted_iota(i32, (256, width), 0)
    before = (row < lax.broadcasted_iota(i32, (256, width), 1)).astype(bf16)
    counting = jnp.concatenate([before, jnp.ones((256, width), bf16)], 1)
    carry = jnp.zeros((256, width), f32)
    ranks = []
    for part in range(leaving // width):
        hit = row == dest[:, part * width : (part + 1) * width]
        counted = jnp.dot(hit.astype(bf16), counting, preferred_element_type=f32)
        ranks.append(jnp.sum(jnp.where(hit, counted[:, :width] + carry, 0.0), 0, keepdims=True))
        carry = carry + counted[:, width:]
    rank = jnp.concatenate(ranks, 1).astype(i32)
    key = (dest // N) * 8 + rank
    picks = (lax.broadcasted_iota(i32, (128, leaving), 0) == key).astype(bf16)
    state = state_ref[...]
    state = jnp.concatenate([state, jnp.zeros((1, leaving), f32)], 0)
    stacked = jnp.concatenate(split3(state), 0)
    lane_bin = dest % N
    chosen = [jnp.where(lane_bin == db, stacked, 0.0) for db in range(N)]
    chosen = jnp.concatenate(chosen, 0).astype(bf16)
    placed = lax.dot_general(chosen, picks, (((1,), (1,)), ((), ())), preferred_element_type=f32)
    for db in range(N):
        base = 24 * db
        out_ref[db] = placed[base : base + 8] + placed[base + 8 : base + 16] + placed[base + 16 : base + 24]


def swap_groups(tiles):
    lane = lax.broadcasted_iota(i32, (8, 128), 1)
    for bit in (1, 2, 4, 8):
        low = (lane // 8) % (2 * bit) < bit
        fresh = list(tiles)
        for a in range(N):
            if a & bit == 0:
                b = a | bit
                fresh[a] = jnp.where(low, tiles[a], pltpu.roll(tiles[b], 8 * bit, 1))
                fresh[b] = jnp.where(low, pltpu.roll(tiles[a], 128 - 8 * bit, 1), tiles[b])
        tiles = fresh
    return tiles


def pair_features(sph):
    width = sph.shape[1]
    position, radius = sph[0:3], sph[6:7]
    base = radius * radius - jnp.sum(position * position, 0, keepdims=True)
    base = jnp.where(radius > 0, base, -1e30)
    high, middle, low = split3(jnp.concatenate([position, radius], 0))
    base = jnp.concatenate(split3(base), 0)
    one = jnp.ones((3, width), f32)
    none = jnp.zeros((2, width), f32)
    left = [2.0 * high, 2.0 * high, 2.0 * middle, 2.0 * middle, 2.0 * high, 2.0 * low, base, one, none]
    right = [high, middle, high, middle, low, high, one, base, none]
    row = lax.broadcasted_iota(i32, sph.shape, 0)
    weighed = jnp.where(row == 6, 1.0, sph)
    high, middle, low = split3(weighed)
    stacked = jnp.concatenate([high, middle, low, jnp.zeros_like(high)], 0)
    return (
        jnp.concatenate(left, 0),
        jnp.concatenate(right, 0).astype(bf16),
        stacked.astype(bf16),
    )


def triangle_features(corner):
    a, e1, e2 = corner[0:3], [corner[3 + k] - corner[k] for k in range(3)], [corner[6 + k] - corner[k] for k in range(3)]
    d11 = e1[0] * e1[0] + e1[1] * e1[1] + e1[2] * e1[2]
    d12 = e1[0] * e2[0] + e1[1] * e2[1] + e1[2] * e2[2]
    d22 = e2[0] * e2[0] + e2[1] * e2[1] + e2[2] * e2[2]
    inverse = 1.0 / (d11 * d22 - d12 * d12)
    for_b = [(d22 * e1[k] - d12 * e2[k]) * inverse for k in range(3)]
    for_c = [(d11 * e2[k] - d12 * e1[k]) * inverse for k in range(3)]
    for g in (for_b, for_c):
        g.append(-(g[0] * a[0] + g[1] * a[1] + g[2] * a[2]))
    return [*a, *e1, *e2], [for_b, for_c]


def set_triangles(sel_ref, plain_ref, linear_ref):
    for entry in range(2):
        for group in range(4):
            corner = []
            for c in range(9):
                at = c * 4 + group
                corner.append(sel_ref[at // 3, entry, at % 3])
            plain, (for_b, for_c) = triangle_features(corner)
            for f, value in enumerate(plain):
                plain_ref[entry, pl.ds(8 * group, 8), f, :] = value
            for k, value in enumerate(for_b + for_c):
                linear_ref[entry, pl.ds(8 * group, 8), k, :] = value


def set_spheres(sph_ref, wide_ref, point_ref):
    one, none = jnp.ones((1, 128), f32), jnp.zeros((1, 128), f32)
    for t in range(sph_ref.shape[0]):
        tile = sph_ref[t]
        high, middle, low = split3(tile[0:3])
        high, middle, low = [high, one, high, one], [middle, none, middle, none], [low, none, low, none]
        rows = jnp.concatenate([*high, *high, *middle, *middle, *high, *low], 0)
        point_ref[t] = rows.T.astype(bf16)
        turned = tile.T
        for f, c in enumerate((0, 1, 2, 6)):
            column = turned[:, c : c + 1]
            if c == 6:
                column = column * column
            wide_ref[t, f] = jnp.broadcast_to(column, (128, 128))


def wall_tiles(code_ref, entry, plain_ref, linear_ref, wide_ref, point_ref, coef_refs, push_refs, sums_ref, adds_ref):
    count = code_ref.shape[1]
    lane = lax.broadcasted_iota(i32, (128, 128), 1)
    upper = lax.broadcasted_iota(i32, (8, 128), 0) < 4

    def tiles_of(n):
        code = code_ref[entry, n]
        return code >> 5, code & 31

    def weigh(n, coef_ref):
        st, tt = tiles_of(n)
        high, middle, low = split3(linear_ref[entry, tt])
        rows = [high, middle, high, middle, low, high]
        for_b = jnp.concatenate([jnp.where(upper, g, 0.0) for g in rows], 0)
        for_c = jnp.concatenate([jnp.where(upper, 0.0, g) for g in rows], 0)
        coefficients = jnp.concatenate([for_b, for_c], 1).astype(bf16)
        points = point_ref[st]
        coef_ref[...] = jnp.dot(points, coefficients, preferred_element_type=f32)

    def push(n, coef_ref, push_ref):
        st, tt = tiles_of(n)
        ax, ay, az, ux, uy, uz, wx, wy, wz = (
            jnp.broadcast_to(plain_ref[entry, tt, f : f + 1, :], (8, 128)) for f in range(9)
        )

        def eight(group):
            here = slice(8 * group, 8 * group + 8)
            b, c = coef_ref[here, 0:128], coef_ref[here, 128:256]
            a = jnp.maximum((1.0 - b) - c, 0.0)
            b = jnp.maximum(b, 0.0)
            c = jnp.maximum(c, 0.0)
            total = a + b + c
            inverse = pl.reciprocal(total, approx=True)
            inverse = inverse * (2.0 - total * inverse)
            b, c = b * inverse, c * inverse
            ox = (wide_ref[st, 0, here, :] - ax) - b * ux - c * wx
            oy = (wide_ref[st, 1, here, :] - ay) - b * uy - c * wy
            oz = (wide_ref[st, 2, here, :] - az) - b * uz - c * wz
            strength = jnp.maximum(wide_ref[st, 3, here, :] - (ox * ox + oy * oy + oz * oz), 0.0)
            return strength * ox, strength * oy, strength * oz

        for group in range(8):
            here = slice(16 * group, 16 * group + 16)
            for k, both in enumerate(zip(eight(2 * group), eight(2 * group + 1))):
                value = jnp.concatenate(both, 0)
                high = value.astype(bf16)
                push_ref[here, 128 * k : 128 * k + 128] = high
                push_ref[here, 384 + 128 * k : 512 + 128 * k] = (value - high.astype(f32)).astype(bf16)

    def add_up(n, push_ref):
        added = jnp.dot(push_ref[...], adds_ref[...], preferred_element_type=f32)
        sums_ref[entry] = jnp.where((lane & 31) == n, added, sums_ref[entry])

    weigh(0, coef_refs[0])
    push_refs[1][...] = jnp.zeros_like(push_refs[1])

    def two_tiles(i, carry):
        n = 2 * i
        weigh(n + 1, coef_refs[1])
        push(n, coef_refs[0], push_refs[0])
        add_up(n - 1, push_refs[1])
        weigh(jnp.minimum(n + 2, count - 1), coef_refs[0])
        push(n + 1, coef_refs[1], push_refs[1])
        add_up(n, push_refs[0])
        return carry

    lax.fori_loop(0, count // 2, two_tiles, 0)
    add_up(count - 1, push_refs[1])


def set_adds(adds_ref):
    block = lax.broadcasted_iota(i32, (6 * 128, 128), 0) >> 7
    block = jnp.where(block < 3, block, block - 3)
    adds_ref[...] = (block == (lax.broadcasted_iota(i32, (6 * 128, 128), 1) >> 5)).astype(bf16)


def set_pairs(sph_ref, left_ref, right_ref, stacked_ref, summed_ref):
    for t in range(sph_ref.shape[0]):
        left, right, stacked = pair_features(sph_ref[t])
        lanes = slice(128 * t, 128 * t + 128)
        left_ref[pl.ds(128 * t, 128), :] = left.T.astype(bf16)
        right_ref[:, lanes], stacked_ref[:, lanes] = right, stacked
    summed_ref[...] = jnp.zeros_like(summed_ref)


def pair_sums(first, last, left_ref, right_ref, stacked_ref, summed_ref):
    rows = 256

    def row_group(step, carry):
        start = pl.multiple_of(step * rows, rows)
        left = left_ref[pl.ds(start, rows), :]
        weighed = stacked_ref[:, pl.ds(start, rows)]
        for column in range(0, right_ref.shape[1], 256):
            here = slice(column, column + 256)
            gap = jnp.dot(left, right_ref[:, here], preferred_element_type=f32)
            inter = jnp.maximum(gap, 0.0)
            high = inter.astype(bf16)
            low = (inter - high.astype(f32)).astype(bf16)
            summed_ref[:, here] += jnp.dot(weighed, high, preferred_element_type=f32) + jnp.dot(
                weighed, low, preferred_element_type=f32
            )
        return carry

    lax.fori_loop(first, last, row_group, 0)


def wall_forces(codes, entry, sums_ref):
    turned = sums_ref[entry].T
    tiles = lax.broadcasted_iota(i32, (16, codes.shape[1]), 0)
    chosen = (tiles == codes >> 5).astype(f32)
    return [
        stiff_wall * jnp.dot(chosen, turned[32 * k : 32 * k + 32], precision=lax.Precision.HIGHEST, preferred_element_type=f32)
        for k in range(3)
    ]


def wrench_line(sph_ref, force):
    tiles = sph_ref.shape[0]
    pos = [jnp.concatenate([sph_ref[t, k : k + 1, :] for t in range(tiles)], 0) for k in range(3)]
    moment = [
        pos[1] * force[2] - pos[2] * force[1],
        pos[2] * force[0] - pos[0] * force[2],
        pos[0] * force[1] - pos[1] * force[0],
    ]
    lane = lax.broadcasted_iota(i32, (1, 128), 1)
    line = jnp.zeros((1, 128), f32)
    for k, value in enumerate(force + moment):
        line = jnp.where(lane == k, -jnp.sum(jnp.sum(value, 0, keepdims=True), 1, keepdims=True), line)
    return line


def set_state(sph_ref, summed_ref, wall, state_out):
    falling = jnp.where(lax.broadcasted_iota(i32, (3, 128), 0) == 2, gravity, 0.0)
    for t in range(sph_ref.shape[0]):
        lanes = slice(128 * t, 128 * t + 128)
        tile = sph_ref[t]
        pos, vel, radius = tile[0:3], tile[3:6], tile[6:7]
        weighted = summed_ref[0:8, lanes] + summed_ref[8:16, lanes] + summed_ref[16:24, lanes]
        totals = weighted[6:7]
        live = radius > 0
        mass = jnp.where(live, radius * radius * radius, 1.0)
        pair = stiff_pair * (totals * pos - weighted[0:3]) - damp_pair * (totals * vel - weighted[3:6])
        push = jnp.concatenate([wall[k][t : t + 1] for k in range(3)], 0)
        fresh = vel + time_step * ((pair + push) / mass - falling)
        block = jnp.concatenate([pos + time_step * fresh, fresh, radius], 0)
        state_out[:, lanes] = jnp.where(live, block, 0.0)


def step_kernel(
    state_hbm, dest_hbm, body_hbm, code_hbm, tri_ref, state_out, kick_out,
    state_ref, dest_ref, body_ref, code_ref, codes_ref,
    out1, got1, out2, sph, piece, sel_send, sel, names, names_got, names_smem,
    wide, point, plain, linear, coef0, coef1, push0, push1, sums, adds, left, right, stacked, summed,
    part, part_got, row, row_got,
    s1, r1, s2, r2, t1s, t1r, ns, nr, t2s, t2r, w1s, w1r, w2s, w2r, own_sem, names_sem,
    in0, in1, in2, in3, in4,
):
    sector, bin_ = lax.axis_index("sector"), lax.axis_index("bin")
    inputs = [
        pltpu.make_async_copy(source, target, semaphore)
        for source, target, semaphore in (
            (dest_hbm, dest_ref, in0),
            (state_hbm, state_ref, in1),
            (body_hbm, body_ref, in2),
            (code_hbm, code_ref, in3),
            (code_hbm, codes_ref, in4),
        )
    ]
    for copy in inputs:
        copy.start()
    barrier = greet(sector, bin_)
    for copy in inputs:
        copy.wait()
    outgoing_tiles(state_ref, dest_ref, out1)
    lane = lax.broadcasted_iota(i32, (1, 128), 1)
    names[...] = jnp.where(lane == 0, body_ref[0, 0], body_ref[0, 1])
    set_adds(adds)
    pl.semaphore_wait(barrier, 2 * (N - 1))

    def along_sector(source, landing, sent, arrived):
        def copy(src, dst):
            return pltpu.make_async_remote_copy(
                src_ref=source(dst), dst_ref=landing(src), send_sem=sent, recv_sem=arrived,
                device_id=(dst, bin_), device_id_type=MESH,
            )

        return copy

    def along_bin(source, landing, sent, arrived):
        def copy(src, dst):
            return pltpu.make_async_remote_copy(
                src_ref=source(dst), dst_ref=landing(src), send_sem=sent, recv_sem=arrived,
                device_id=(sector, dst), device_id_type=MESH,
            )

        return copy

    def peers(me):
        return [lax.rem(me + off, N) for off in range(1, N)]

    def all_of(buffer, count, semaphore):
        view = buffer.at[pl.ds(0, count)]
        pltpu.make_async_copy(view, view, semaphore).wait()

    sphere_one = along_bin(lambda d: out1.at[d], lambda s: got1.at[s], s1, r1)
    sphere_two = along_sector(lambda d: out2.at[d], lambda s: sph.at[s], s2, r2)
    piece_one = along_sector(lambda d: tri_ref.at[pl.ds(3 * piece_of(d), 3)], lambda s: piece.at[s], t1s, t1r)
    names_one = along_sector(lambda d: names, lambda s: names_got.at[s], ns, nr)
    piece_two = along_sector(lambda d: sel_send.at[d], lambda s: sel.at[piece_of(s)], t2s, t2r)
    wrench_one = along_sector(lambda d: part.at[d], lambda s: part_got.at[s], w1s, w1r)
    wrench_two = along_bin(lambda d: row, lambda s: row_got.at[s], w2s, w2r)

    holding = is_holder(sector)
    for peer in peers(bin_):
        sphere_one(bin_, peer).start()
    for peer in peers(sector):

        @pl.when(is_holder(peer))
        def _(peer=peer):
            names_one(sector, peer).start()
            piece_one(sector, peer).start()

    @pl.when(holding)
    def _():
        own = pltpu.make_async_copy(tri_ref.at[pl.ds(3 * piece_of(sector), 3)], piece.at[sector], own_sem)
        own.start()
        names_got[sector] = names[...]
        own.wait()

    got1[bin_] = out1[bin_]
    all_of(got1, N - 1, r1)
    for ds, tile in enumerate(swap_groups([got1[sb] for sb in range(N)])):
        out2[ds] = tile
    for peer in peers(sector):
        sphere_two(sector, peer).start()
    sph[sector] = out2[sector]

    @pl.when(holding)
    def _():
        all_of(names_got, N - 1, nr)
        listed = pltpu.make_async_copy(names_got, names_smem, names_sem)
        listed.start()
        all_of(piece, N - 1, t1r)
        listed.wait()
        for dst in range(N):
            for entry in range(2):
                sel_send[dst, entry] = piece[names_smem[dst, 0, entry]]
        for peer in peers(sector):
            piece_two(sector, peer).start()
        sel[piece_of(sector)] = sel_send[sector]

    all_of(sph, N - 1, r2)
    set_spheres(sph, wide, point)
    set_pairs(sph, left, right, stacked, summed)
    pair_sums(0, PAIRS_ONE, left, right, stacked, summed)

    @pl.when(holding)
    def _():
        all_of(sel, HOLDERS - 1, t2r)

    @pl.when(jnp.logical_not(holding))
    def _():
        all_of(sel, HOLDERS, t2r)

    set_triangles(sel, plain, linear)
    body_row = lax.broadcasted_iota(i32, (N, 1, 128), 0)
    parts = jnp.zeros((N, 1, 128), f32)
    wall = [jnp.zeros((16, 128), f32)] * 3
    for entry in range(2):
        sums[entry] = jnp.zeros((128, 128), f32)
        wall_tiles(code_ref, entry, plain, linear, wide, point, (coef0, coef1), (push0, push1), sums, adds)
        force = wall_forces(codes_ref[entry : entry + 1, :], entry, sums)
        wall = [w + g for w, g in zip(wall, force)]
        parts = parts + jnp.where(body_row == body_ref[0, entry], wrench_line(sph, force)[None], 0.0)
    part[...] = parts

    for peer in peers(sector):
        wrench_one(sector, peer).start()
    part_got[sector] = part[sector]
    pair_sums(PAIRS_ONE, PAIRS_TWO, left, right, stacked, summed)
    all_of(part_got, N - 1, w1r)
    row[...] = functools.reduce(jnp.add, [part_got[k] for k in range(N)])
    for peer in peers(bin_):
        wrench_two(bin_, peer).start()
    row_got[bin_] = row[...]
    pair_sums(PAIRS_TWO, PAIRS_ALL, left, right, stacked, summed)
    set_state(sph, summed, wall, state_out)
    all_of(row_got, N - 1, w2r)
    total = functools.reduce(jnp.add, [row_got[k] for k in range(N)])
    total = total * jnp.where(lane < 3, time_step / body_mass, time_step / body_inertia)
    kick_out[...] = total[:, 0:6]

    all_of(out1, N - 1, s1)
    all_of(out2, N - 1, s2)
    all_of(part, N - 1, w1s)
    all_of(row_got, N - 1, w2s)

    @pl.when(holding)
    def _():
        all_of(names_got, HOLDERS - 1, ns)
        all_of(piece, HOLDERS - 1, t1s)
        all_of(sel_send, N - 1, t2s)

    @pl.when(jnp.logical_not(holding))
    def _():
        all_of(names_got, HOLDERS, ns)
        all_of(piece, HOLDERS, t1s)


PAIRS_ONE, PAIRS_TWO, PAIRS_ALL = 3, 6, 8


def step(state, dest, bodies, codes, tri):
    slots = 2 * state.shape[1]
    vmem = pl.BlockSpec(memory_space=pltpu.VMEM)
    dma = pltpu.SemaphoreType.DMA
    line = pltpu.VMEM((N, 1, 128), f32)
    tiles = pltpu.VMEM((N, 8, 128), f32)
    return pl.pallas_call(
        step_kernel,
        out_shape=(jax.ShapeDtypeStruct((7, slots), f32), jax.ShapeDtypeStruct((1, 6), f32)),
        in_specs=[pl.BlockSpec(memory_space=pltpu.HBM)] * 5,
        out_specs=(vmem, vmem),
        scratch_shapes=[
            pltpu.VMEM(state.shape, f32),
            pltpu.VMEM(dest.shape, i32),
            pltpu.SMEM(bodies.shape, i32),
            pltpu.SMEM(codes.shape, i32),
            pltpu.VMEM(codes.shape, i32),
            *[tiles] * 4,
            pltpu.VMEM((N, 3, 8, 128), f32),
            pltpu.VMEM((N, 2, 3, 8, 128), f32),
            pltpu.VMEM((HOLDERS, 2, 3, 8, 128), f32),
            pltpu.VMEM((1, 128), i32),
            pltpu.VMEM((N, 1, 128), i32),
            pltpu.SMEM((N, 1, 128), i32),
            pltpu.VMEM((N, 4, 128, 128), f32),
            pltpu.VMEM((N, 128, 48), bf16),
            pltpu.VMEM((2, 32, 16, 128), f32),
            pltpu.VMEM((2, 32, 8, 128), f32),
            pltpu.VMEM((128, 256), f32),
            pltpu.VMEM((128, 256), f32),
            pltpu.VMEM((128, 768), bf16),
            pltpu.VMEM((128, 768), bf16),
            pltpu.VMEM((2, 128, 128), f32),
            pltpu.VMEM((768, 128), bf16),
            pltpu.VMEM((slots, 32), bf16),
            pltpu.VMEM((32, slots), bf16),
            pltpu.VMEM((32, slots), bf16),
            pltpu.VMEM((32, slots), f32),
            line,
            line,
            pltpu.VMEM((1, 128), f32),
            line,
        ]
        + [dma] * 21,
        compiler_params=pltpu.CompilerParams(collective_id=0, has_side_effects=True, vmem_limit_bytes=60 * 2**20),
    )(state, dest, bodies, codes, tri)


def local(sph_state, sph_dest, body_list, tile_codes, triangles):
    dest = sph_dest.reshape(1, -1)
    tri = triangles.reshape(36, 8, 128)
    return step(sph_state, dest, body_list, tile_codes[0], tri)


def solution(mesh):
    return jax.shard_map(
        local,
        mesh=mesh,
        in_specs=(
            P(None, ("sector", "bin")),
            P(("sector", "bin"), None),
            P(("sector", "bin"), None),
            P(("sector", "bin"), None, None),
            P(None, "sector", "bin"),
        ),
        out_specs=(P(None, ("sector", "bin")), P("sector", None)),
        check_vma=False,
    )
```

```python
import functools

import jax
import jax.numpy as jnp
from jax import lax
from jax.experimental import pallas as pl
from jax.experimental.pallas import tpu as pltpu
from jax.sharding import PartitionSpec as P

stiff_pair = 50.0
damp_pair = 2.0
stiff_wall = 50.0
time_step = 0.01
gravity = 9.81
body_mass = 4.0
body_inertia = 40.0

MESH = pl.DeviceIdType.MESH
N = 16
HOLDERS = 12
f32, bf16, i32 = jnp.float32, jnp.bfloat16, jnp.int32


def split3(value):
    high = value.astype(bf16).astype(f32)
    rest = value - high
    middle = rest.astype(bf16).astype(f32)
    return high, middle, rest - middle


def is_holder(s):
    return (s // 4) != (s % 4)


def piece_of(s):
    y, x = s // 4, s % 4
    return 3 * y + x - jnp.where(x > y, 1, 0)


def holder_at(piece):
    y, x = piece // 3, piece % 3
    return 4 * y + x + (1 if x >= y else 0)


def greet(sector, bin_):
    barrier = pltpu.get_barrier_semaphore()
    for off in range(1, N):
        pl.semaphore_signal(barrier, inc=1, device_id=(sector, lax.rem(bin_ + off, N)), device_id_type=MESH)
        pl.semaphore_signal(barrier, inc=1, device_id=(lax.rem(sector + off, N), bin_), device_id_type=MESH)
    return barrier


def outgoing_tiles(state_ref, dest_ref, out_ref):
    leaving = state_ref.shape[1]
    dest = dest_ref[...]
    width = 256
    row = lax.broadcasted_iota(i32, (256, width), 0)
    before = (row < lax.broadcasted_iota(i32, (256, width), 1)).astype(bf16)
    counting = jnp.concatenate([before, jnp.ones((256, width), bf16)], 1)
    carry = jnp.zeros((256, width), f32)
    ranks = []
    for part in range(leaving // width):
        hit = row == dest[:, part * width : (part + 1) * width]
        counted = jnp.dot(hit.astype(bf16), counting, preferred_element_type=f32)
        ranks.append(jnp.sum(jnp.where(hit, counted[:, :width] + carry, 0.0), 0, keepdims=True))
        carry = carry + counted[:, width:]
    rank = jnp.concatenate(ranks, 1).astype(i32)
    key = (dest // N) * 8 + rank
    picks = (lax.broadcasted_iota(i32, (128, leaving), 0) == key).astype(bf16)
    state = state_ref[...]
    state = jnp.concatenate([state, jnp.zeros((1, leaving), f32)], 0)
    stacked = jnp.concatenate(split3(state), 0)
    lane_bin = dest % N
    chosen = [jnp.where(lane_bin == db, stacked, 0.0) for db in range(N)]
    chosen = jnp.concatenate(chosen, 0).astype(bf16)
    placed = lax.dot_general(chosen, picks, (((1,), (1,)), ((), ())), preferred_element_type=f32)
    for db in range(N):
        base = 24 * db
        out_ref[db] = placed[base : base + 8] + placed[base + 8 : base + 16] + placed[base + 16 : base + 24]


def swap_groups(tiles):
    lane = lax.broadcasted_iota(i32, (8, 128), 1)
    for bit in (1, 2, 4, 8):
        low = (lane // 8) % (2 * bit) < bit
        fresh = list(tiles)
        for a in range(N):
            if a & bit == 0:
                b = a | bit
                fresh[a] = jnp.where(low, tiles[a], pltpu.roll(tiles[b], 8 * bit, 1))
                fresh[b] = jnp.where(low, pltpu.roll(tiles[a], 128 - 8 * bit, 1), tiles[b])
        tiles = fresh
    return tiles


def pair_features(sph):
    width = sph.shape[1]
    position, radius = sph[0:3], sph[6:7]
    base = radius * radius - jnp.sum(position * position, 0, keepdims=True)
    base = jnp.where(radius > 0, base, -1e30)
    high, middle, low = split3(jnp.concatenate([position, radius], 0))
    base = jnp.concatenate(split3(base), 0)
    one = jnp.ones((3, width), f32)
    none = jnp.zeros((2, width), f32)
    left = [2.0 * high, 2.0 * high, 2.0 * middle, 2.0 * middle, 2.0 * high, 2.0 * low, base, one, none]
    right = [high, middle, high, middle, low, high, one, base, none]
    row = lax.broadcasted_iota(i32, sph.shape, 0)
    weighed = jnp.where(row == 6, 1.0, sph)
    high, middle, low = split3(weighed)
    stacked = jnp.concatenate([high, middle, low, jnp.zeros_like(high)], 0)
    return (
        jnp.concatenate(left, 0),
        jnp.concatenate(right, 0).astype(bf16),
        stacked.astype(bf16),
    )


def triangle_features(corner):
    a, e1, e2 = corner[0:3], [corner[3 + k] - corner[k] for k in range(3)], [corner[6 + k] - corner[k] for k in range(3)]
    d11 = e1[0] * e1[0] + e1[1] * e1[1] + e1[2] * e1[2]
    d12 = e1[0] * e2[0] + e1[1] * e2[1] + e1[2] * e2[2]
    d22 = e2[0] * e2[0] + e2[1] * e2[1] + e2[2] * e2[2]
    inverse = 1.0 / (d11 * d22 - d12 * d12)
    for_b = [(d22 * e1[k] - d12 * e2[k]) * inverse for k in range(3)]
    for_c = [(d11 * e2[k] - d12 * e1[k]) * inverse for k in range(3)]
    for g in (for_b, for_c):
        g.append(-(g[0] * a[0] + g[1] * a[1] + g[2] * a[2]))
    return [*a, *e1, *e2], [for_b, for_c]


def set_triangles(sel_ref, plain_ref, linear_ref):
    for entry in range(2):
        for group in range(4):
            corner = []
            for c in range(9):
                at = c * 4 + group
                corner.append(sel_ref[at // 3, entry, at % 3])
            plain, (for_b, for_c) = triangle_features(corner)
            for f, value in enumerate(plain):
                plain_ref[entry, pl.ds(8 * group, 8), f, :] = value
            for k, value in enumerate(for_b + for_c):
                linear_ref[entry, pl.ds(8 * group, 8), k, :] = value


def set_spheres(sph_ref, wide_ref, point_ref):
    one, none = jnp.ones((1, 128), f32), jnp.zeros((1, 128), f32)
    for t in range(sph_ref.shape[0]):
        tile = sph_ref[t]
        high, middle, low = split3(tile[0:3])
        high, middle, low = [high, one, high, one], [middle, none, middle, none], [low, none, low, none]
        rows = jnp.concatenate([*high, *high, *middle, *middle, *high, *low], 0)
        point_ref[t] = rows.T.astype(bf16)
        turned = tile.T
        for f, c in enumerate((0, 1, 2, 6)):
            column = turned[:, c : c + 1]
            if c == 6:
                column = column * column
            wide_ref[t, f] = jnp.broadcast_to(column, (128, 128))


def wall_tiles(code_ref, entry, plain_ref, linear_ref, wide_ref, point_ref, coef_refs, slot_ref, order_ref):
    count = code_ref.shape[1]
    upper = lax.broadcasted_iota(i32, (8, 128), 0) < 4

    def tiles_of(n):
        code = code_ref[entry, n]
        return code >> 5, code & 31

    def weigh(n, coef_ref):
        st, tt = tiles_of(n)
        high, middle, low = split3(linear_ref[entry, tt])
        rows = [high, middle, high, middle, low, high]
        for_b = jnp.concatenate([jnp.where(upper, g, 0.0) for g in rows], 0)
        for_c = jnp.concatenate([jnp.where(upper, 0.0, g) for g in rows], 0)
        coefficients = jnp.concatenate([for_b, for_c], 1).astype(bf16)
        points = point_ref[st]
        coef_ref[...] = jnp.dot(points, coefficients, preferred_element_type=f32)

    def push(n, coef_ref):
        st, tt = tiles_of(n)
        before = order_ref[entry, n]
        ax, ay, az, ux, uy, uz, wx, wy, wz = (
            jnp.broadcast_to(plain_ref[entry, tt, f : f + 1, :], (8, 128)) for f in range(9)
        )

        def eight(group):
            here = slice(8 * group, 8 * group + 8)
            b, c = coef_ref[here, 0:128], coef_ref[here, 128:256]
            a = jnp.maximum((1.0 - b) - c, 0.0)
            b = jnp.maximum(b, 0.0)
            c = jnp.maximum(c, 0.0)
            total = a + b + c
            inverse = pl.reciprocal(total, approx=True)
            inverse = inverse * (2.0 - total * inverse)
            b, c = b * inverse, c * inverse
            ox = (wide_ref[st, 0, here, :] - ax) - b * ux - c * wx
            oy = (wide_ref[st, 1, here, :] - ay) - b * uy - c * wy
            oz = (wide_ref[st, 2, here, :] - az) - b * uz - c * wz
            strength = jnp.maximum(wide_ref[st, 3, here, :] - (ox * ox + oy * oy + oz * oz), 0.0)
            return strength * ox, strength * oy, strength * oz

        def held(first):
            return [[slot_ref[entry, before, k, 8 * g : 8 * g + 8, :] for k in range(3)] for g in range(first, first + 2)]

        for first in range(0, 16, 2):
            earlier = held(first)
            for g in range(2):
                here = slice(8 * (first + g), 8 * (first + g) + 8)
                for k, value in enumerate(eight(first + g)):
                    slot_ref[entry, n, k, here, :] = earlier[g][k] + value

    weigh(0, coef_refs[0])

    def two_tiles(i, carry):
        n = 2 * i
        weigh(n + 1, coef_refs[1])
        push(n, coef_refs[0])
        weigh(jnp.minimum(n + 2, count - 1), coef_refs[0])
        push(n + 1, coef_refs[1])
        return carry

    lax.fori_loop(0, count // 2, two_tiles, 0)


def set_order(code_ref, order_ref):
    count = code_ref.shape[1]
    row = lax.broadcasted_iota(i32, (count, 128), 0)
    lane = lax.broadcasted_iota(i32, (count, 128), 1)

    def latest(hit):
        found = jnp.where(hit, row, -1)
        found = functools.reduce(jnp.maximum, [found[8 * g : 8 * g + 8] for g in range(count // 8)])
        for shift in (4, 2, 1):
            found = jnp.maximum(found, pltpu.roll(found, shift, 0))
        return jnp.where(found < 0, count, found)[0:1]

    for entry in range(2):
        down, along = jnp.zeros((count, 128), i32), jnp.full((count, 128), -1, i32)
        for n in range(count):
            tile = code_ref[entry, n] >> 5
            down = jnp.where(row == n, tile, down)
            along = jnp.where(lane == n, tile, along)
        order_ref[entry : entry + 1, :] = latest((down == along) & (row < lane))
        order_ref[2 + entry : 3 + entry, :] = latest(down == lane)


def set_adds(adds_ref):
    block = lax.broadcasted_iota(i32, (6 * 128, 128), 0) >> 7
    block = jnp.where(block < 3, block, block - 3)
    adds_ref[...] = (block == (lax.broadcasted_iota(i32, (6 * 128, 128), 1) >> 5)).astype(bf16)


def set_pairs(sph_ref, left_ref, right_ref, stacked_ref, summed_ref):
    for t in range(sph_ref.shape[0]):
        left, right, stacked = pair_features(sph_ref[t])
        lanes = slice(128 * t, 128 * t + 128)
        left_ref[pl.ds(128 * t, 128), :] = left.T.astype(bf16)
        right_ref[:, lanes], stacked_ref[:, lanes] = right, stacked
    summed_ref[...] = jnp.zeros_like(summed_ref)


def pair_sums(first, last, left_ref, right_ref, stacked_ref, summed_ref):
    rows = 256

    def row_group(step, carry):
        start = pl.multiple_of(step * rows, rows)
        left = left_ref[pl.ds(start, rows), :]
        weighed = stacked_ref[:, pl.ds(start, rows)]
        for column in range(0, right_ref.shape[1], 256):
            here = slice(column, column + 256)
            gap = jnp.dot(left, right_ref[:, here], preferred_element_type=f32)
            inter = jnp.maximum(gap, 0.0)
            high = inter.astype(bf16)
            low = (inter - high.astype(f32)).astype(bf16)
            summed_ref[:, here] += jnp.dot(weighed, high, preferred_element_type=f32) + jnp.dot(
                weighed, low, preferred_element_type=f32
            )
        return carry

    lax.fori_loop(first, last, row_group, 0)


def wall_forces(slot_ref, order_ref, sums_ref, adds_ref):
    lane = lax.broadcasted_iota(i32, (128, 128), 1) & 31
    sums_ref[...] = jnp.zeros_like(sums_ref)

    def four_tiles(i, carry):
        for st in [4 * i + k for k in range(4)]:
            last = [order_ref[2 + entry, st] for entry in range(2)]
            highs, lows = [], []
            for k in range(3):
                value = slot_ref[0, last[0], k] + slot_ref[1, last[1], k]
                high = value.astype(bf16)
                highs.append(high)
                lows.append((value - high.astype(f32)).astype(bf16))
            added = jnp.dot(jnp.concatenate(highs + lows, 1), adds_ref[...], preferred_element_type=f32)
            sums_ref[...] = jnp.where(lane == st, added, sums_ref[...])
        return carry

    lax.fori_loop(0, 4, four_tiles, 0)
    turned = sums_ref[...].T
    return [stiff_wall * turned[32 * k : 32 * k + 16] for k in range(3)]


def wrench_line(entry, slot_ref, order_ref, wide_ref):
    def one_tile(st, carry):
        last = order_ref[2 + entry, st]
        total = list(carry)
        for group in range(16):
            here = slice(8 * group, 8 * group + 8)
            x, y, z = (slot_ref[entry, last, k, here, :] for k in range(3))
            px, py, pz = (wide_ref[st, k, here, :] for k in range(3))
            moment = (py * z - pz * y, pz * x - px * z, px * y - py * x)
            total = [t + value for t, value in zip(total, (x, y, z, *moment))]
        return tuple(total)

    total = lax.fori_loop(0, 16, one_tile, (jnp.zeros((8, 128), f32),) * 6)
    lane = lax.broadcasted_iota(i32, (1, 128), 1)
    line = jnp.zeros((1, 128), f32)
    for k, value in enumerate(total):
        value = jnp.sum(jnp.sum(value, 0, keepdims=True), 1, keepdims=True)
        line = jnp.where(lane == k, -stiff_wall * value, line)
    return line


def set_state(sph_ref, summed_ref, wall, state_out):
    falling = jnp.where(lax.broadcasted_iota(i32, (3, 128), 0) == 2, gravity, 0.0)
    for t in range(sph_ref.shape[0]):
        lanes = slice(128 * t, 128 * t + 128)
        tile = sph_ref[t]
        pos, vel, radius = tile[0:3], tile[3:6], tile[6:7]
        weighted = summed_ref[0:8, lanes] + summed_ref[8:16, lanes] + summed_ref[16:24, lanes]
        totals = weighted[6:7]
        live = radius > 0
        mass = jnp.where(live, radius * radius * radius, 1.0)
        pair = stiff_pair * (totals * pos - weighted[0:3]) - damp_pair * (totals * vel - weighted[3:6])
        push = jnp.concatenate([wall[k][t : t + 1] for k in range(3)], 0)
        fresh = vel + time_step * ((pair + push) / mass - falling)
        block = jnp.concatenate([pos + time_step * fresh, fresh, radius], 0)
        state_out[:, lanes] = jnp.where(live, block, 0.0)


def step_kernel(
    state_hbm, dest_hbm, body_hbm, code_hbm, tri_ref, state_out, kick_out,
    state_ref, dest_ref, body_ref, code_ref,
    out1, got1, out2, sph, piece, sel_send, sel, names, names_got, names_smem,
    wide, point, plain, linear, coef0, coef1, slots, sums, adds, order, order_smem, left, right, stacked, summed,
    part, part_got, row, row_got,
    s1, r1, s2, r2, t1s, t1r, ns, nr, t2s, t2r, w1s, w1r, w2s, w2r, own_sem, names_sem,
    in0, in1, in2, in3, in4,
):
    sector, bin_ = lax.axis_index("sector"), lax.axis_index("bin")
    inputs = [
        pltpu.make_async_copy(source, target, semaphore)
        for source, target, semaphore in (
            (dest_hbm, dest_ref, in0),
            (state_hbm, state_ref, in1),
            (body_hbm, body_ref, in2),
            (code_hbm, code_ref, in3),
        )
    ]
    for copy in inputs:
        copy.start()
    barrier = greet(sector, bin_)
    for copy in inputs:
        copy.wait()
    outgoing_tiles(state_ref, dest_ref, out1)
    lane = lax.broadcasted_iota(i32, (1, 128), 1)
    names[...] = jnp.where(lane == 0, body_ref[0, 0], body_ref[0, 1])
    set_adds(adds)
    for entry in range(2):
        slots[entry, 32] = jnp.zeros((3, 128, 128), f32)
    set_order(code_ref, order)
    ordered = pltpu.make_async_copy(order, order_smem, in4)
    ordered.start()
    ordered.wait()
    pl.semaphore_wait(barrier, 2 * (N - 1))

    def along_sector(source, landing, sent, arrived):
        def copy(src, dst):
            return pltpu.make_async_remote_copy(
                src_ref=source(dst), dst_ref=landing(src), send_sem=sent, recv_sem=arrived,
                device_id=(dst, bin_), device_id_type=MESH,
            )

        return copy

    def along_bin(source, landing, sent, arrived):
        def copy(src, dst):
            return pltpu.make_async_remote_copy(
                src_ref=source(dst), dst_ref=landing(src), send_sem=sent, recv_sem=arrived,
                device_id=(sector, dst), device_id_type=MESH,
            )

        return copy

    def peers(me):
        return [lax.rem(me + off, N) for off in range(1, N)]

    def all_of(buffer, count, semaphore):
        view = buffer.at[pl.ds(0, count)]
        pltpu.make_async_copy(view, view, semaphore).wait()

    sphere_one = along_bin(lambda d: out1.at[d], lambda s: got1.at[s], s1, r1)
    sphere_two = along_sector(lambda d: out2.at[d], lambda s: sph.at[s], s2, r2)
    piece_one = along_sector(lambda d: tri_ref.at[pl.ds(3 * piece_of(d), 3)], lambda s: piece.at[s], t1s, t1r)
    names_one = along_sector(lambda d: names, lambda s: names_got.at[s], ns, nr)
    piece_two = along_sector(lambda d: sel_send.at[d], lambda s: sel.at[piece_of(s)], t2s, t2r)
    wrench_one = along_sector(lambda d: part.at[d], lambda s: part_got.at[s], w1s, w1r)
    wrench_two = along_bin(lambda d: row, lambda s: row_got.at[s], w2s, w2r)

    holding = is_holder(sector)
    for peer in peers(bin_):
        sphere_one(bin_, peer).start()
    for peer in peers(sector):

        @pl.when(is_holder(peer))
        def _(peer=peer):
            names_one(sector, peer).start()
            piece_one(sector, peer).start()

    @pl.when(holding)
    def _():
        own = pltpu.make_async_copy(tri_ref.at[pl.ds(3 * piece_of(sector), 3)], piece.at[sector], own_sem)
        own.start()
        names_got[sector] = names[...]
        own.wait()

    got1[bin_] = out1[bin_]
    all_of(got1, N - 1, r1)
    for ds, tile in enumerate(swap_groups([got1[sb] for sb in range(N)])):
        out2[ds] = tile
    for peer in peers(sector):
        sphere_two(sector, peer).start()
    sph[sector] = out2[sector]

    @pl.when(holding)
    def _():
        all_of(names_got, N - 1, nr)
        listed = pltpu.make_async_copy(names_got, names_smem, names_sem)
        listed.start()
        all_of(piece, N - 1, t1r)
        listed.wait()
        for dst in range(N):
            for entry in range(2):
                sel_send[dst, entry] = piece[names_smem[dst, 0, entry]]
        for peer in peers(sector):
            piece_two(sector, peer).start()
        sel[piece_of(sector)] = sel_send[sector]

    all_of(sph, N - 1, r2)
    set_spheres(sph, wide, point)
    set_pairs(sph, left, right, stacked, summed)
    pair_sums(0, PAIRS_ONE, left, right, stacked, summed)

    @pl.when(holding)
    def _():
        all_of(sel, HOLDERS - 1, t2r)

    @pl.when(jnp.logical_not(holding))
    def _():
        all_of(sel, HOLDERS, t2r)

    set_triangles(sel, plain, linear)
    body_row = lax.broadcasted_iota(i32, (N, 1, 128), 0)
    parts = jnp.zeros((N, 1, 128), f32)
    for entry in range(2):
        wall_tiles(code_ref, entry, plain, linear, wide, point, (coef0, coef1), slots, order_smem)
        parts = parts + jnp.where(body_row == body_ref[0, entry], wrench_line(entry, slots, order_smem, wide)[None], 0.0)
    part[...] = parts

    for peer in peers(sector):
        wrench_one(sector, peer).start()
    part_got[sector] = part[sector]
    wall = wall_forces(slots, order_smem, sums, adds)
    pair_sums(PAIRS_ONE, PAIRS_TWO, left, right, stacked, summed)
    all_of(part_got, N - 1, w1r)
    row[...] = functools.reduce(jnp.add, [part_got[k] for k in range(N)])
    for peer in peers(bin_):
        wrench_two(bin_, peer).start()
    row_got[bin_] = row[...]
    pair_sums(PAIRS_TWO, PAIRS_ALL, left, right, stacked, summed)
    set_state(sph, summed, wall, state_out)
    all_of(row_got, N - 1, w2r)
    total = functools.reduce(jnp.add, [row_got[k] for k in range(N)])
    total = total * jnp.where(lane < 3, time_step / body_mass, time_step / body_inertia)
    kick_out[...] = total[:, 0:6]

    all_of(out1, N - 1, s1)
    all_of(out2, N - 1, s2)
    all_of(part, N - 1, w1s)
    all_of(row_got, N - 1, w2s)

    @pl.when(holding)
    def _():
        all_of(names_got, HOLDERS - 1, ns)
        all_of(piece, HOLDERS - 1, t1s)
        all_of(sel_send, N - 1, t2s)

    @pl.when(jnp.logical_not(holding))
    def _():
        all_of(names_got, HOLDERS, ns)
        all_of(piece, HOLDERS, t1s)


PAIRS_ONE, PAIRS_TWO, PAIRS_ALL = 3, 5, 8


def step(state, dest, bodies, codes, tri):
    slots = 2 * state.shape[1]
    vmem = pl.BlockSpec(memory_space=pltpu.VMEM)
    dma = pltpu.SemaphoreType.DMA
    line = pltpu.VMEM((N, 1, 128), f32)
    tiles = pltpu.VMEM((N, 8, 128), f32)
    return pl.pallas_call(
        step_kernel,
        out_shape=(jax.ShapeDtypeStruct((7, slots), f32), jax.ShapeDtypeStruct((1, 6), f32)),
        in_specs=[pl.BlockSpec(memory_space=pltpu.HBM)] * 5,
        out_specs=(vmem, vmem),
        scratch_shapes=[
            pltpu.VMEM(state.shape, f32),
            pltpu.VMEM(dest.shape, i32),
            pltpu.SMEM(bodies.shape, i32),
            pltpu.SMEM(codes.shape, i32),
            *[tiles] * 4,
            pltpu.VMEM((N, 3, 8, 128), f32),
            pltpu.VMEM((N, 2, 3, 8, 128), f32),
            pltpu.VMEM((HOLDERS, 2, 3, 8, 128), f32),
            pltpu.VMEM((1, 128), i32),
            pltpu.VMEM((N, 1, 128), i32),
            pltpu.SMEM((N, 1, 128), i32),
            pltpu.VMEM((N, 4, 128, 128), f32),
            pltpu.VMEM((N, 128, 48), bf16),
            pltpu.VMEM((2, 32, 16, 128), f32),
            pltpu.VMEM((2, 32, 8, 128), f32),
            pltpu.VMEM((128, 256), f32),
            pltpu.VMEM((128, 256), f32),
            pltpu.VMEM((2, 33, 3, 128, 128), f32),
            pltpu.VMEM((128, 128), f32),
            pltpu.VMEM((768, 128), bf16),
            pltpu.VMEM((4, 128), i32),
            pltpu.SMEM((4, 128), i32),
            pltpu.VMEM((slots, 32), bf16),
            pltpu.VMEM((32, slots), bf16),
            pltpu.VMEM((32, slots), bf16),
            pltpu.VMEM((32, slots), f32),
            line,
            line,
            pltpu.VMEM((1, 128), f32),
            line,
        ]
        + [dma] * 21,
        compiler_params=pltpu.CompilerParams(collective_id=0, has_side_effects=True, vmem_limit_bytes=60 * 2**20),
    )(state, dest, bodies, codes, tri)


def local(sph_state, sph_dest, body_list, tile_codes, triangles):
    dest = sph_dest.reshape(1, -1)
    tri = triangles.reshape(36, 8, 128)
    return step(sph_state, dest, body_list, tile_codes[0], tri)


def solution(mesh):
    return jax.shard_map(
        local,
        mesh=mesh,
        in_specs=(
            P(None, ("sector", "bin")),
            P(("sector", "bin"), None),
            P(("sector", "bin"), None),
            P(("sector", "bin"), None, None),
            P(None, "sector", "bin"),
        ),
        out_specs=(P(None, ("sector", "bin")), P("sector", None)),
        check_vma=False,
    )
```

```python
import functools

import jax
import jax.numpy as jnp
from jax import lax
from jax.experimental import pallas as pl
from jax.experimental.pallas import tpu as pltpu
from jax.sharding import PartitionSpec as P

stiff_pair = 50.0
damp_pair = 2.0
stiff_wall = 50.0
time_step = 0.01
gravity = 9.81
body_mass = 4.0
body_inertia = 40.0

MESH = pl.DeviceIdType.MESH
N = 16
HOLDERS = 12
f32, bf16, i32 = jnp.float32, jnp.bfloat16, jnp.int32


def split3(value):
    high = value.astype(bf16).astype(f32)
    rest = value - high
    middle = rest.astype(bf16).astype(f32)
    return high, middle, rest - middle


def is_holder(s):
    return (s // 4) != (s % 4)


def piece_of(s):
    y, x = s // 4, s % 4
    return 3 * y + x - jnp.where(x > y, 1, 0)


def holder_at(piece):
    y, x = piece // 3, piece % 3
    return 4 * y + x + (1 if x >= y else 0)


def greet(sector, bin_):
    barrier = pltpu.get_barrier_semaphore()
    for off in range(1, N):
        pl.semaphore_signal(barrier, inc=1, device_id=(sector, lax.rem(bin_ + off, N)), device_id_type=MESH)
        pl.semaphore_signal(barrier, inc=1, device_id=(lax.rem(sector + off, N), bin_), device_id_type=MESH)
    return barrier


def outgoing_tiles(state_ref, dest_ref, out_ref):
    leaving = state_ref.shape[1]
    dest = dest_ref[...]
    width = 256
    row = lax.broadcasted_iota(i32, (256, width), 0)
    before = (row < lax.broadcasted_iota(i32, (256, width), 1)).astype(bf16)
    counting = jnp.concatenate([before, jnp.ones((256, width), bf16)], 1)
    carry = jnp.zeros((256, width), f32)
    ranks = []
    for part in range(leaving // width):
        hit = row == dest[:, part * width : (part + 1) * width]
        counted = jnp.dot(hit.astype(bf16), counting, preferred_element_type=f32)
        ranks.append(jnp.sum(jnp.where(hit, counted[:, :width] + carry, 0.0), 0, keepdims=True))
        carry = carry + counted[:, width:]
    rank = jnp.concatenate(ranks, 1).astype(i32)
    key = (dest // N) * 8 + rank
    picks = (lax.broadcasted_iota(i32, (128, leaving), 0) == key).astype(bf16)
    state = state_ref[...]
    state = jnp.concatenate([state, jnp.zeros((1, leaving), f32)], 0)
    stacked = jnp.concatenate(split3(state), 0)
    lane_bin = dest % N
    chosen = [jnp.where(lane_bin == db, stacked, 0.0) for db in range(N)]
    chosen = jnp.concatenate(chosen, 0).astype(bf16)
    placed = lax.dot_general(chosen, picks, (((1,), (1,)), ((), ())), preferred_element_type=f32)
    for db in range(N):
        base = 24 * db
        out_ref[db] = placed[base : base + 8] + placed[base + 8 : base + 16] + placed[base + 16 : base + 24]


def swap_groups(tiles):
    lane = lax.broadcasted_iota(i32, (8, 128), 1)
    for bit in (1, 2, 4, 8):
        low = (lane // 8) % (2 * bit) < bit
        fresh = list(tiles)
        for a in range(N):
            if a & bit == 0:
                b = a | bit
                fresh[a] = jnp.where(low, tiles[a], pltpu.roll(tiles[b], 8 * bit, 1))
                fresh[b] = jnp.where(low, pltpu.roll(tiles[a], 128 - 8 * bit, 1), tiles[b])
        tiles = fresh
    return tiles


def pair_features(sph):
    width = sph.shape[1]
    position, radius = sph[0:3], sph[6:7]
    base = radius * radius - jnp.sum(position * position, 0, keepdims=True)
    base = jnp.where(radius > 0, base, -1e30)
    high, middle, low = split3(jnp.concatenate([position, radius], 0))
    base = jnp.concatenate(split3(base), 0)
    one = jnp.ones((3, width), f32)
    none = jnp.zeros((2, width), f32)
    left = [2.0 * high, 2.0 * high, 2.0 * middle, 2.0 * middle, 2.0 * high, 2.0 * low, base, one, none]
    right = [high, middle, high, middle, low, high, one, base, none]
    row = lax.broadcasted_iota(i32, sph.shape, 0)
    weighed = jnp.where(row == 6, 1.0, sph)
    high, middle, low = split3(weighed)
    stacked = jnp.concatenate([high, middle, low, jnp.zeros_like(high)], 0)
    return (
        jnp.concatenate(left, 0),
        jnp.concatenate(right, 0).astype(bf16),
        stacked.astype(bf16),
    )


def triangle_features(corner):
    a, e1, e2 = corner[0:3], [corner[3 + k] - corner[k] for k in range(3)], [corner[6 + k] - corner[k] for k in range(3)]
    d11 = e1[0] * e1[0] + e1[1] * e1[1] + e1[2] * e1[2]
    d12 = e1[0] * e2[0] + e1[1] * e2[1] + e1[2] * e2[2]
    d22 = e2[0] * e2[0] + e2[1] * e2[1] + e2[2] * e2[2]
    inverse = 1.0 / (d11 * d22 - d12 * d12)
    for_b = [(d22 * e1[k] - d12 * e2[k]) * inverse for k in range(3)]
    for_c = [(d11 * e2[k] - d12 * e1[k]) * inverse for k in range(3)]
    for g in (for_b, for_c):
        g.append(-(g[0] * a[0] + g[1] * a[1] + g[2] * a[2]))
    return [*a, *e1, *e2], [for_b, for_c]


def set_triangles(sel_ref, plain_ref, linear_ref):
    for entry in range(2):
        for group in range(4):
            corner = []
            for c in range(9):
                at = c * 4 + group
                corner.append(sel_ref[at // 3, entry, at % 3])
            plain, (for_b, for_c) = triangle_features(corner)
            for f, value in enumerate(plain):
                plain_ref[entry, pl.ds(8 * group, 8), f, :] = value
            for k, value in enumerate(for_b + for_c):
                linear_ref[entry, pl.ds(8 * group, 8), k, :] = value


def set_spheres(sph_ref, wide_ref, point_ref):
    one, none = jnp.ones((1, 128), f32), jnp.zeros((1, 128), f32)
    for t in range(sph_ref.shape[0]):
        tile = sph_ref[t]
        high, middle, low = split3(tile[0:3])
        high, middle, low = [high, one, high, one], [middle, none, middle, none], [low, none, low, none]
        rows = jnp.concatenate([*high, *high, *middle, *middle, *high, *low], 0)
        point_ref[t] = rows.T.astype(bf16)
        turned = tile.T
        for f, c in enumerate((0, 1, 2, 6)):
            column = turned[:, c : c + 1]
            if c == 6:
                column = column * column
            wide_ref[t, f] = jnp.broadcast_to(column, (128, 128))


def wall_tiles(code_ref, entry, plain_ref, linear_ref, wide_ref, point_ref, coef_refs, slot_ref, order_ref):
    count = code_ref.shape[1]
    upper = lax.broadcasted_iota(i32, (8, 128), 0) < 4

    def tiles_of(n):
        code = code_ref[entry, n]
        return code >> 5, code & 31

    def weigh(n, coef_ref):
        st, tt = tiles_of(n)
        high, middle, low = split3(linear_ref[entry, tt])
        rows = [high, middle, high, middle, low, high]
        for_b = jnp.concatenate([jnp.where(upper, g, 0.0) for g in rows], 0)
        for_c = jnp.concatenate([jnp.where(upper, 0.0, g) for g in rows], 0)
        coefficients = jnp.concatenate([for_b, for_c], 1).astype(bf16)
        points = point_ref[st]
        coef_ref[...] = jnp.dot(points, coefficients, preferred_element_type=f32)

    def push(n, coef_ref):
        st, tt = tiles_of(n)
        before = order_ref[entry, n]
        ax, ay, az, ux, uy, uz, wx, wy, wz = (
            jnp.broadcast_to(plain_ref[entry, tt, f : f + 1, :], (8, 128)) for f in range(9)
        )

        def eight(group):
            here = slice(8 * group, 8 * group + 8)
            b, c = coef_ref[here, 0:128], coef_ref[here, 128:256]
            a = jnp.maximum((1.0 - b) - c, 0.0)
            b = jnp.maximum(b, 0.0)
            c = jnp.maximum(c, 0.0)
            total = a + b + c
            inverse = pl.reciprocal(total, approx=True)
            b, c = b * inverse, c * inverse
            ox = (wide_ref[st, 0, here, :] - ax) - b * ux - c * wx
            oy = (wide_ref[st, 1, here, :] - ay) - b * uy - c * wy
            oz = (wide_ref[st, 2, here, :] - az) - b * uz - c * wz
            strength = jnp.maximum(wide_ref[st, 3, here, :] - (ox * ox + oy * oy + oz * oz), 0.0)
            return strength * ox, strength * oy, strength * oz

        def held(first):
            return [[slot_ref[entry, before, k, 8 * g : 8 * g + 8, :] for k in range(3)] for g in range(first, first + 2)]

        for first in range(0, 16, 2):
            earlier = held(first)
            for g in range(2):
                here = slice(8 * (first + g), 8 * (first + g) + 8)
                for k, value in enumerate(eight(first + g)):
                    slot_ref[entry, n, k, here, :] = earlier[g][k] + value

    weigh(0, coef_refs[0])

    def two_tiles(i, carry):
        n = 2 * i
        weigh(n + 1, coef_refs[1])
        push(n, coef_refs[0])
        weigh(jnp.minimum(n + 2, count - 1), coef_refs[0])
        push(n + 1, coef_refs[1])
        return carry

    lax.fori_loop(0, count // 2, two_tiles, 0)


def set_order(code_ref, order_ref):
    count = code_ref.shape[1]
    row = lax.broadcasted_iota(i32, (count, 128), 0)
    lane = lax.broadcasted_iota(i32, (count, 128), 1)

    def latest(hit):
        found = jnp.where(hit, row, -1)
        found = functools.reduce(jnp.maximum, [found[8 * g : 8 * g + 8] for g in range(count // 8)])
        for shift in (4, 2, 1):
            found = jnp.maximum(found, pltpu.roll(found, shift, 0))
        return jnp.where(found < 0, count, found)[0:1]

    for entry in range(2):
        down, along = jnp.zeros((count, 128), i32), jnp.full((count, 128), -1, i32)
        for n in range(count):
            tile = code_ref[entry, n] >> 5
            down = jnp.where(row == n, tile, down)
            along = jnp.where(lane == n, tile, along)
        order_ref[entry : entry + 1, :] = latest((down == along) & (row < lane))
        order_ref[2 + entry : 3 + entry, :] = latest(down == lane)


def set_adds(adds_ref):
    block = lax.broadcasted_iota(i32, (6 * 128, 128), 0) >> 7
    block = jnp.where(block < 3, block, block - 3)
    adds_ref[...] = (block == (lax.broadcasted_iota(i32, (6 * 128, 128), 1) >> 5)).astype(bf16)


def set_pairs(sph_ref, left_ref, right_ref, stacked_ref, summed_ref):
    for t in range(sph_ref.shape[0]):
        left, right, stacked = pair_features(sph_ref[t])
        lanes = slice(128 * t, 128 * t + 128)
        left_ref[pl.ds(128 * t, 128), :] = left.T.astype(bf16)
        right_ref[:, lanes], stacked_ref[:, lanes] = right, stacked
    summed_ref[...] = jnp.zeros_like(summed_ref)


def pair_sums(first, last, left_ref, right_ref, stacked_ref, summed_ref):
    rows = 256

    def row_group(step, carry):
        start = pl.multiple_of(step * rows, rows)
        left = left_ref[pl.ds(start, rows), :]
        weighed = stacked_ref[:, pl.ds(start, rows)]
        for column in range(0, right_ref.shape[1], 256):
            here = slice(column, column + 256)
            gap = jnp.dot(left, right_ref[:, here], preferred_element_type=f32)
            inter = jnp.maximum(gap, 0.0)
            high = inter.astype(bf16)
            low = (inter - high.astype(f32)).astype(bf16)
            summed_ref[:, here] += jnp.dot(weighed, high, preferred_element_type=f32) + jnp.dot(
                weighed, low, preferred_element_type=f32
            )
        return carry

    lax.fori_loop(first, last, row_group, 0)


def wall_forces(slot_ref, order_ref, sums_ref, adds_ref):
    lane = lax.broadcasted_iota(i32, (128, 128), 1) & 31
    sums_ref[...] = jnp.zeros_like(sums_ref)

    def four_tiles(i, carry):
        for st in [4 * i + k for k in range(4)]:
            last = [order_ref[2 + entry, st] for entry in range(2)]
            highs, lows = [], []
            for k in range(3):
                value = slot_ref[0, last[0], k] + slot_ref[1, last[1], k]
                high = value.astype(bf16)
                highs.append(high)
                lows.append((value - high.astype(f32)).astype(bf16))
            added = jnp.dot(jnp.concatenate(highs + lows, 1), adds_ref[...], preferred_element_type=f32)
            sums_ref[...] = jnp.where(lane == st, added, sums_ref[...])
        return carry

    lax.fori_loop(0, 4, four_tiles, 0)
    turned = sums_ref[...].T
    return [stiff_wall * turned[32 * k : 32 * k + 16] for k in range(3)]


def wrench_line(entry, slot_ref, order_ref, wide_ref):
    def one_tile(st, carry):
        last = order_ref[2 + entry, st]
        total = list(carry)
        for group in range(16):
            here = slice(8 * group, 8 * group + 8)
            x, y, z = (slot_ref[entry, last, k, here, :] for k in range(3))
            px, py, pz = (wide_ref[st, k, here, :] for k in range(3))
            moment = (py * z - pz * y, pz * x - px * z, px * y - py * x)
            total = [t + value for t, value in zip(total, (x, y, z, *moment))]
        return tuple(total)

    total = lax.fori_loop(0, 16, one_tile, (jnp.zeros((8, 128), f32),) * 6)
    lane = lax.broadcasted_iota(i32, (1, 128), 1)
    line = jnp.zeros((1, 128), f32)
    for k, value in enumerate(total):
        value = jnp.sum(jnp.sum(value, 0, keepdims=True), 1, keepdims=True)
        line = jnp.where(lane == k, -stiff_wall * value, line)
    return line


def set_state(sph_ref, summed_ref, wall, state_out):
    falling = jnp.where(lax.broadcasted_iota(i32, (3, 128), 0) == 2, gravity, 0.0)
    for t in range(sph_ref.shape[0]):
        lanes = slice(128 * t, 128 * t + 128)
        tile = sph_ref[t]
        pos, vel, radius = tile[0:3], tile[3:6], tile[6:7]
        weighted = summed_ref[0:8, lanes] + summed_ref[8:16, lanes] + summed_ref[16:24, lanes]
        totals = weighted[6:7]
        live = radius > 0
        mass = jnp.where(live, radius * radius * radius, 1.0)
        pair = stiff_pair * (totals * pos - weighted[0:3]) - damp_pair * (totals * vel - weighted[3:6])
        push = jnp.concatenate([wall[k][t : t + 1] for k in range(3)], 0)
        fresh = vel + time_step * ((pair + push) / mass - falling)
        block = jnp.concatenate([pos + time_step * fresh, fresh, radius], 0)
        state_out[:, lanes] = jnp.where(live, block, 0.0)


def step_kernel(
    state_hbm, dest_hbm, body_hbm, code_hbm, tri_ref, state_out, kick_out,
    state_ref, dest_ref, body_ref, code_ref,
    out1, got1, out2, sph, piece, sel_send, sel, names, names_got, names_smem,
    wide, point, plain, linear, coef0, coef1, slots, sums, adds, order, order_smem, left, right, stacked, summed,
    part, part_got, row, row_got,
    s1, r1, s2, r2, t1s, t1r, ns, nr, t2s, t2r, w1s, w1r, w2s, w2r, own_sem, names_sem,
    in0, in1, in2, in3, in4,
):
    sector, bin_ = lax.axis_index("sector"), lax.axis_index("bin")
    inputs = [
        pltpu.make_async_copy(source, target, semaphore)
        for source, target, semaphore in (
            (dest_hbm, dest_ref, in0),
            (state_hbm, state_ref, in1),
            (body_hbm, body_ref, in2),
            (code_hbm, code_ref, in3),
        )
    ]
    for copy in inputs:
        copy.start()
    barrier = greet(sector, bin_)
    for copy in inputs:
        copy.wait()
    outgoing_tiles(state_ref, dest_ref, out1)
    lane = lax.broadcasted_iota(i32, (1, 128), 1)
    names[...] = jnp.where(lane == 0, body_ref[0, 0], body_ref[0, 1])
    set_adds(adds)
    for entry in range(2):
        slots[entry, 32] = jnp.zeros((3, 128, 128), f32)
    set_order(code_ref, order)
    ordered = pltpu.make_async_copy(order, order_smem, in4)
    ordered.start()
    ordered.wait()
    pl.semaphore_wait(barrier, 2 * (N - 1))

    def along_sector(source, landing, sent, arrived):
        def copy(src, dst):
            return pltpu.make_async_remote_copy(
                src_ref=source(dst), dst_ref=landing(src), send_sem=sent, recv_sem=arrived,
                device_id=(dst, bin_), device_id_type=MESH,
            )

        return copy

    def along_bin(source, landing, sent, arrived):
        def copy(src, dst):
            return pltpu.make_async_remote_copy(
                src_ref=source(dst), dst_ref=landing(src), send_sem=sent, recv_sem=arrived,
                device_id=(sector, dst), device_id_type=MESH,
            )

        return copy

    def peers(me):
        return [lax.rem(me + off, N) for off in range(1, N)]

    def all_of(buffer, count, semaphore):
        view = buffer.at[pl.ds(0, count)]
        pltpu.make_async_copy(view, view, semaphore).wait()

    sphere_one = along_bin(lambda d: out1.at[d], lambda s: got1.at[s], s1, r1)
    sphere_two = along_sector(lambda d: out2.at[d], lambda s: sph.at[s], s2, r2)
    piece_one = along_sector(lambda d: tri_ref.at[pl.ds(3 * piece_of(d), 3)], lambda s: piece.at[s], t1s, t1r)
    names_one = along_sector(lambda d: names, lambda s: names_got.at[s], ns, nr)
    piece_two = along_sector(lambda d: sel_send.at[d], lambda s: sel.at[piece_of(s)], t2s, t2r)
    wrench_one = along_sector(lambda d: part.at[d], lambda s: part_got.at[s], w1s, w1r)
    wrench_two = along_bin(lambda d: row, lambda s: row_got.at[s], w2s, w2r)

    holding = is_holder(sector)
    for peer in peers(bin_):
        sphere_one(bin_, peer).start()
    for peer in peers(sector):

        @pl.when(is_holder(peer))
        def _(peer=peer):
            names_one(sector, peer).start()
            piece_one(sector, peer).start()

    @pl.when(holding)
    def _():
        own = pltpu.make_async_copy(tri_ref.at[pl.ds(3 * piece_of(sector), 3)], piece.at[sector], own_sem)
        own.start()
        names_got[sector] = names[...]
        own.wait()
        all_of(names_got, N - 1, nr)
        pltpu.make_async_copy(names_got, names_smem, names_sem).start()

    got1[bin_] = out1[bin_]
    all_of(got1, N - 1, r1)
    for ds, tile in enumerate(swap_groups([got1[sb] for sb in range(N)])):
        out2[ds] = tile
    for peer in peers(sector):
        sphere_two(sector, peer).start()
    sph[sector] = out2[sector]

    @pl.when(holding)
    def _():
        all_of(piece, N - 1, t1r)
        pltpu.make_async_copy(names_got, names_smem, names_sem).wait()
        for dst in range(N):
            for entry in range(2):
                sel_send[dst, entry] = piece[names_smem[dst, 0, entry]]
        for peer in peers(sector):
            piece_two(sector, peer).start()
        sel[piece_of(sector)] = sel_send[sector]

    all_of(sph, N - 1, r2)
    set_spheres(sph, wide, point)
    set_pairs(sph, left, right, stacked, summed)
    pair_sums(0, PAIRS_ONE, left, right, stacked, summed)

    @pl.when(holding)
    def _():
        all_of(sel, HOLDERS - 1, t2r)

    @pl.when(jnp.logical_not(holding))
    def _():
        all_of(sel, HOLDERS, t2r)

    set_triangles(sel, plain, linear)
    body_row = lax.broadcasted_iota(i32, (N, 1, 128), 0)
    parts = jnp.zeros((N, 1, 128), f32)
    for entry in range(2):
        wall_tiles(code_ref, entry, plain, linear, wide, point, (coef0, coef1), slots, order_smem)
        parts = parts + jnp.where(body_row == body_ref[0, entry], wrench_line(entry, slots, order_smem, wide)[None], 0.0)
    part[...] = parts

    for peer in peers(sector):
        wrench_one(sector, peer).start()
    part_got[sector] = part[sector]
    wall = wall_forces(slots, order_smem, sums, adds)
    pair_sums(PAIRS_ONE, PAIRS_TWO, left, right, stacked, summed)
    all_of(part_got, N - 1, w1r)
    row[...] = functools.reduce(jnp.add, [part_got[k] for k in range(N)])
    for peer in peers(bin_):
        wrench_two(bin_, peer).start()
    row_got[bin_] = row[...]
    pair_sums(PAIRS_TWO, PAIRS_ALL, left, right, stacked, summed)
    set_state(sph, summed, wall, state_out)
    all_of(row_got, N - 1, w2r)
    total = functools.reduce(jnp.add, [row_got[k] for k in range(N)])
    total = total * jnp.where(lane < 3, time_step / body_mass, time_step / body_inertia)
    kick_out[...] = total[:, 0:6]

    all_of(out1, N - 1, s1)
    all_of(out2, N - 1, s2)
    all_of(part, N - 1, w1s)
    all_of(row_got, N - 1, w2s)

    @pl.when(holding)
    def _():
        all_of(names_got, HOLDERS - 1, ns)
        all_of(piece, HOLDERS - 1, t1s)
        all_of(sel_send, N - 1, t2s)

    @pl.when(jnp.logical_not(holding))
    def _():
        all_of(names_got, HOLDERS, ns)
        all_of(piece, HOLDERS, t1s)


PAIRS_ONE, PAIRS_TWO, PAIRS_ALL = 1, 4, 8


def step(state, dest, bodies, codes, tri):
    slots = 2 * state.shape[1]
    vmem = pl.BlockSpec(memory_space=pltpu.VMEM)
    dma = pltpu.SemaphoreType.DMA
    line = pltpu.VMEM((N, 1, 128), f32)
    tiles = pltpu.VMEM((N, 8, 128), f32)
    return pl.pallas_call(
        step_kernel,
        out_shape=(pltpu.VMEM((7, slots), f32), pltpu.VMEM((1, 6), f32)),
        in_specs=[pl.BlockSpec(memory_space=pltpu.HBM)] * 5,
        out_specs=(vmem, vmem),
        scratch_shapes=[
            pltpu.VMEM(state.shape, f32),
            pltpu.VMEM(dest.shape, i32),
            pltpu.SMEM(bodies.shape, i32),
            pltpu.SMEM(codes.shape, i32),
            *[tiles] * 4,
            pltpu.VMEM((N, 3, 8, 128), f32),
            pltpu.VMEM((N, 2, 3, 8, 128), f32),
            pltpu.VMEM((HOLDERS, 2, 3, 8, 128), f32),
            pltpu.VMEM((1, 128), i32),
            pltpu.VMEM((N, 1, 128), i32),
            pltpu.SMEM((N, 1, 128), i32),
            pltpu.VMEM((N, 4, 128, 128), f32),
            pltpu.VMEM((N, 128, 48), bf16),
            pltpu.VMEM((2, 32, 16, 128), f32),
            pltpu.VMEM((2, 32, 8, 128), f32),
            pltpu.VMEM((128, 256), f32),
            pltpu.VMEM((128, 256), f32),
            pltpu.VMEM((2, 33, 3, 128, 128), f32),
            pltpu.VMEM((128, 128), f32),
            pltpu.VMEM((768, 128), bf16),
            pltpu.VMEM((4, 128), i32),
            pltpu.SMEM((4, 128), i32),
            pltpu.VMEM((slots, 32), bf16),
            pltpu.VMEM((32, slots), bf16),
            pltpu.VMEM((32, slots), bf16),
            pltpu.VMEM((32, slots), f32),
            line,
            line,
            pltpu.VMEM((1, 128), f32),
            line,
        ]
        + [dma] * 21,
        compiler_params=pltpu.CompilerParams(collective_id=0, has_side_effects=True, vmem_limit_bytes=60 * 2**20),
    )(state, dest, bodies, codes, tri)


def local(sph_state, sph_dest, body_list, tile_codes, triangles):
    dest = sph_dest.reshape(1, -1)
    tri = triangles.reshape(36, 8, 128)
    return step(sph_state, dest, body_list, tile_codes[0], tri)


def solution(mesh):
    return jax.shard_map(
        local,
        mesh=mesh,
        in_specs=(
            P(None, ("sector", "bin")),
            P(("sector", "bin"), None),
            P(("sector", "bin"), None),
            P(("sector", "bin"), None, None),
            P(None, "sector", "bin"),
        ),
        out_specs=(P(None, ("sector", "bin")), P("sector", None)),
        check_vma=False,
    )
```

```python
import functools

import jax
import jax.numpy as jnp
from jax import lax
from jax.experimental import pallas as pl
from jax.experimental.pallas import tpu as pltpu
from jax.sharding import PartitionSpec as P

stiff_pair = 50.0
damp_pair = 2.0
stiff_wall = 50.0
time_step = 0.01
gravity = 9.81
body_mass = 4.0
body_inertia = 40.0

MESH = pl.DeviceIdType.MESH
N = 16
HOLDERS = 12
f32, bf16, i32 = jnp.float32, jnp.bfloat16, jnp.int32


def split3(value):
    high = value.astype(bf16).astype(f32)
    rest = value - high
    middle = rest.astype(bf16).astype(f32)
    return high, middle, rest - middle


def is_holder(s):
    return (s // 4) != (s % 4)


def piece_of(s):
    y, x = s // 4, s % 4
    return 3 * y + x - jnp.where(x > y, 1, 0)


def holder_at(piece):
    y, x = piece // 3, piece % 3
    return 4 * y + x + (1 if x >= y else 0)


def greet(sector, bin_):
    barrier = pltpu.get_barrier_semaphore()
    for off in range(1, N):
        pl.semaphore_signal(barrier, inc=1, device_id=(sector, lax.rem(bin_ + off, N)), device_id_type=MESH)
        pl.semaphore_signal(barrier, inc=1, device_id=(lax.rem(sector + off, N), bin_), device_id_type=MESH)
    return barrier


def outgoing_tiles(state_ref, dest_ref, out_ref):
    leaving = state_ref.shape[1]
    dest = dest_ref[...]
    width = 256
    row = lax.broadcasted_iota(i32, (256, width), 0)
    before = (row < lax.broadcasted_iota(i32, (256, width), 1)).astype(bf16)
    counting = jnp.concatenate([before, jnp.ones((256, width), bf16)], 1)
    carry = jnp.zeros((256, width), f32)
    ranks = []
    for part in range(leaving // width):
        hit = row == dest[:, part * width : (part + 1) * width]
        counted = jnp.dot(hit.astype(bf16), counting, preferred_element_type=f32)
        ranks.append(jnp.sum(jnp.where(hit, counted[:, :width] + carry, 0.0), 0, keepdims=True))
        carry = carry + counted[:, width:]
    rank = jnp.concatenate(ranks, 1).astype(i32)
    key = (dest // N) * 8 + rank
    picks = (lax.broadcasted_iota(i32, (128, leaving), 0) == key).astype(bf16)
    state = state_ref[...]
    state = jnp.concatenate([state, jnp.zeros((1, leaving), f32)], 0)
    stacked = jnp.concatenate(split3(state), 0)
    lane_bin = dest % N
    chosen = [jnp.where(lane_bin == db, stacked, 0.0) for db in range(N)]
    chosen = jnp.concatenate(chosen, 0).astype(bf16)
    placed = lax.dot_general(chosen, picks, (((1,), (1,)), ((), ())), preferred_element_type=f32)
    for db in range(N):
        base = 24 * db
        out_ref[db] = placed[base : base + 8] + placed[base + 8 : base + 16] + placed[base + 16 : base + 24]


def swap_groups(tiles):
    lane = lax.broadcasted_iota(i32, (8, 128), 1)
    for bit in (1, 2, 4, 8):
        low = (lane // 8) % (2 * bit) < bit
        fresh = list(tiles)
        for a in range(N):
            if a & bit == 0:
                b = a | bit
                fresh[a] = jnp.where(low, tiles[a], pltpu.roll(tiles[b], 8 * bit, 1))
                fresh[b] = jnp.where(low, pltpu.roll(tiles[a], 128 - 8 * bit, 1), tiles[b])
        tiles = fresh
    return tiles


def pair_features(sph):
    width = sph.shape[1]
    position, radius = sph[0:3], sph[6:7]
    base = radius * radius - jnp.sum(position * position, 0, keepdims=True)
    base = jnp.where(radius > 0, base, -1e30)
    high, middle, low = split3(jnp.concatenate([position, radius], 0))
    base = jnp.concatenate(split3(base), 0)
    one = jnp.ones((3, width), f32)
    none = jnp.zeros((2, width), f32)
    left = [2.0 * high, 2.0 * high, 2.0 * middle, 2.0 * middle, 2.0 * high, 2.0 * low, base, one, none]
    right = [high, middle, high, middle, low, high, one, base, none]
    row = lax.broadcasted_iota(i32, sph.shape, 0)
    weighed = jnp.where(row == 6, 1.0, sph)
    high, middle, low = split3(weighed)
    stacked = jnp.concatenate([high, middle, low, jnp.zeros_like(high)], 0)
    return (
        jnp.concatenate(left, 0),
        jnp.concatenate(right, 0).astype(bf16),
        stacked.astype(bf16),
    )


def triangle_features(corner):
    a, e1, e2 = corner[0:3], [corner[3 + k] - corner[k] for k in range(3)], [corner[6 + k] - corner[k] for k in range(3)]
    d11 = e1[0] * e1[0] + e1[1] * e1[1] + e1[2] * e1[2]
    d12 = e1[0] * e2[0] + e1[1] * e2[1] + e1[2] * e2[2]
    d22 = e2[0] * e2[0] + e2[1] * e2[1] + e2[2] * e2[2]
    inverse = 1.0 / (d11 * d22 - d12 * d12)
    for_b = [(d22 * e1[k] - d12 * e2[k]) * inverse for k in range(3)]
    for_c = [(d11 * e2[k] - d12 * e1[k]) * inverse for k in range(3)]
    for g in (for_b, for_c):
        g.append(-(g[0] * a[0] + g[1] * a[1] + g[2] * a[2]))
    return [*a, *e1, *e2], [for_b, for_c]


def set_triangles(sel_ref, plain_ref, linear_ref):
    for entry in range(2):
        for group in range(4):
            corner = []
            for c in range(9):
                at = c * 4 + group
                corner.append(sel_ref[at // 3, entry, at % 3])
            plain, (for_b, for_c) = triangle_features(corner)
            for f, value in enumerate(plain):
                plain_ref[entry, pl.ds(8 * group, 8), f, :] = value
            for k, value in enumerate(for_b + for_c):
                linear_ref[entry, pl.ds(8 * group, 8), k, :] = value


def set_spheres(sph_ref, wide_ref, point_ref):
    one, none = jnp.ones((1, 128), f32), jnp.zeros((1, 128), f32)
    for t in range(sph_ref.shape[0]):
        tile = sph_ref[t]
        high, middle, low = split3(tile[0:3])
        high, middle, low = [high, one, high, one], [middle, none, middle, none], [low, none, low, none]
        rows = jnp.concatenate([*high, *high, *middle, *middle, *high, *low], 0)
        point_ref[t] = rows.T.astype(bf16)
        turned = tile.T
        for f, c in enumerate((0, 1, 2, 6)):
            column = turned[:, c : c + 1]
            if c == 6:
                column = column * column
            wide_ref[t, f] = jnp.broadcast_to(column, (128, 128))


def wall_tiles(code_ref, plain_ref, linear_ref, wide_ref, point_ref, coef_refs, slot_refs, order_ref):
    count = code_ref.shape[1]
    upper = lax.broadcasted_iota(i32, (8, 128), 0) < 4

    def tiles_of(entry, n):
        code = code_ref[entry, n]
        return code >> 5, code & 31

    def weigh(entry, n, coef_ref):
        st, tt = tiles_of(entry, n)
        high, middle, low = split3(linear_ref[entry, tt])
        rows = [high, middle, high, middle, low, high]
        for_b = jnp.concatenate([jnp.where(upper, g, 0.0) for g in rows], 0)
        for_c = jnp.concatenate([jnp.where(upper, 0.0, g) for g in rows], 0)
        coefficients = jnp.concatenate([for_b, for_c], 1).astype(bf16)
        points = point_ref[st]
        coef_ref[...] = jnp.dot(points, coefficients, preferred_element_type=f32)

    def push(entry, n, coef_ref):
        slot_ref = slot_refs[entry]
        st, tt = tiles_of(entry, n)
        before = order_ref[entry, n]
        ax, ay, az, ux, uy, uz, wx, wy, wz = (
            jnp.broadcast_to(plain_ref[entry, tt, f : f + 1, :], (8, 128)) for f in range(9)
        )

        def eight(group):
            here = slice(8 * group, 8 * group + 8)
            b, c = coef_ref[here, 0:128], coef_ref[here, 128:256]
            a = jnp.maximum((1.0 - b) - c, 0.0)
            b = jnp.maximum(b, 0.0)
            c = jnp.maximum(c, 0.0)
            total = a + b + c
            inverse = pl.reciprocal(total, approx=True)
            b, c = b * inverse, c * inverse
            ox = (wide_ref[st, 0, here, :] - ax) - b * ux - c * wx
            oy = (wide_ref[st, 1, here, :] - ay) - b * uy - c * wy
            oz = (wide_ref[st, 2, here, :] - az) - b * uz - c * wz
            strength = jnp.maximum(wide_ref[st, 3, here, :] - (ox * ox + oy * oy + oz * oz), 0.0)
            return strength * ox, strength * oy, strength * oz

        def held(first):
            return [[slot_ref[before, k, 8 * g : 8 * g + 8, :] for k in range(3)] for g in range(first, first + 2)]

        for first in range(0, 16, 2):
            earlier = held(first)
            for g in range(2):
                here = slice(8 * (first + g), 8 * (first + g) + 8)
                for k, value in enumerate(eight(first + g)):
                    slot_ref[n, k, here, :] = earlier[g][k] + value

    for entry in range(2):
        weigh(entry, 0, coef_refs[entry])

    def two_tiles(i, carry):
        n = 2 * i
        for entry in range(2):
            weigh(entry, n + 1, coef_refs[2 + entry])
        for entry in range(2):
            push(entry, n, coef_refs[entry])
        for entry in range(2):
            weigh(entry, jnp.minimum(n + 2, count - 1), coef_refs[entry])
        for entry in range(2):
            push(entry, n + 1, coef_refs[2 + entry])
        return carry

    lax.fori_loop(0, count // 2, two_tiles, 0)


def set_order(code_ref, order_ref):
    count = code_ref.shape[1]
    row = lax.broadcasted_iota(i32, (count, 128), 0)
    lane = lax.broadcasted_iota(i32, (count, 128), 1)

    def latest(hit):
        found = jnp.where(hit, row, -1)
        found = functools.reduce(jnp.maximum, [found[8 * g : 8 * g + 8] for g in range(count // 8)])
        for shift in (4, 2, 1):
            found = jnp.maximum(found, pltpu.roll(found, shift, 0))
        return jnp.where(found < 0, count, found)[0:1]

    for entry in range(2):
        down, along = jnp.zeros((count, 128), i32), jnp.full((count, 128), -1, i32)
        for n in range(count):
            tile = code_ref[entry, n] >> 5
            down = jnp.where(row == n, tile, down)
            along = jnp.where(lane == n, tile, along)
        order_ref[entry : entry + 1, :] = latest((down == along) & (row < lane))
        order_ref[2 + entry : 3 + entry, :] = latest(down == lane)


def set_adds(adds_ref):
    block = lax.broadcasted_iota(i32, (6 * 128, 128), 0) >> 7
    block = jnp.where(block < 3, block, block - 3)
    adds_ref[...] = (block == (lax.broadcasted_iota(i32, (6 * 128, 128), 1) >> 5)).astype(bf16)


def set_pairs(sph_ref, left_ref, right_ref, stacked_ref, summed_ref):
    for t in range(sph_ref.shape[0]):
        left, right, stacked = pair_features(sph_ref[t])
        lanes = slice(128 * t, 128 * t + 128)
        left_ref[pl.ds(128 * t, 128), :] = left.T.astype(bf16)
        right_ref[:, lanes], stacked_ref[:, lanes] = right, stacked
    summed_ref[...] = jnp.zeros_like(summed_ref)


def pair_sums(first, last, left_ref, right_ref, stacked_ref, summed_ref):
    rows = 256

    def row_group(step, carry):
        start = pl.multiple_of(step * rows, rows)
        left = left_ref[pl.ds(start, rows), :]
        weighed = stacked_ref[:, pl.ds(start, rows)]
        for column in range(0, right_ref.shape[1], 256):
            here = slice(column, column + 256)
            gap = jnp.dot(left, right_ref[:, here], preferred_element_type=f32)
            inter = jnp.maximum(gap, 0.0)
            high = inter.astype(bf16)
            low = (inter - high.astype(f32)).astype(bf16)
            summed_ref[:, here] += jnp.dot(weighed, high, preferred_element_type=f32) + jnp.dot(
                weighed, low, preferred_element_type=f32
            )
        return carry

    lax.fori_loop(first, last, row_group, 0)


def wall_forces(slot_refs, order_ref, sums_ref, adds_ref):
    lane = lax.broadcasted_iota(i32, (128, 128), 1) & 31
    sums_ref[...] = jnp.zeros_like(sums_ref)

    def four_tiles(i, carry):
        for st in [4 * i + k for k in range(4)]:
            last = [order_ref[2 + entry, st] for entry in range(2)]
            highs, lows = [], []
            for k in range(3):
                value = slot_refs[0][last[0], k] + slot_refs[1][last[1], k]
                high = value.astype(bf16)
                highs.append(high)
                lows.append((value - high.astype(f32)).astype(bf16))
            added = jnp.dot(jnp.concatenate(highs + lows, 1), adds_ref[...], preferred_element_type=f32)
            sums_ref[...] = jnp.where(lane == st, added, sums_ref[...])
        return carry

    lax.fori_loop(0, 4, four_tiles, 0)
    turned = sums_ref[...].T
    return [stiff_wall * turned[32 * k : 32 * k + 16] for k in range(3)]


def wrench_line(entry, slot_ref, order_ref, wide_ref):
    def one_tile(st, carry):
        last = order_ref[2 + entry, st]
        total = list(carry)
        for group in range(16):
            here = slice(8 * group, 8 * group + 8)
            x, y, z = (slot_ref[last, k, here, :] for k in range(3))
            px, py, pz = (wide_ref[st, k, here, :] for k in range(3))
            moment = (py * z - pz * y, pz * x - px * z, px * y - py * x)
            total = [t + value for t, value in zip(total, (x, y, z, *moment))]
        return tuple(total)

    total = lax.fori_loop(0, 16, one_tile, (jnp.zeros((8, 128), f32),) * 6)
    lane = lax.broadcasted_iota(i32, (1, 128), 1)
    line = jnp.zeros((1, 128), f32)
    for k, value in enumerate(total):
        value = jnp.sum(jnp.sum(value, 0, keepdims=True), 1, keepdims=True)
        line = jnp.where(lane == k, -stiff_wall * value, line)
    return line


def set_state(sph_ref, summed_ref, wall, state_out):
    falling = jnp.where(lax.broadcasted_iota(i32, (3, 128), 0) == 2, gravity, 0.0)
    for t in range(sph_ref.shape[0]):
        lanes = slice(128 * t, 128 * t + 128)
        tile = sph_ref[t]
        pos, vel, radius = tile[0:3], tile[3:6], tile[6:7]
        weighted = summed_ref[0:8, lanes] + summed_ref[8:16, lanes] + summed_ref[16:24, lanes]
        totals = weighted[6:7]
        live = radius > 0
        mass = jnp.where(live, radius * radius * radius, 1.0)
        pair = stiff_pair * (totals * pos - weighted[0:3]) - damp_pair * (totals * vel - weighted[3:6])
        push = jnp.concatenate([wall[k][t : t + 1] for k in range(3)], 0)
        fresh = vel + time_step * ((pair + push) / mass - falling)
        block = jnp.concatenate([pos + time_step * fresh, fresh, radius], 0)
        state_out[:, lanes] = jnp.where(live, block, 0.0)


def step_kernel(
    state_hbm, dest_hbm, body_hbm, code_hbm, tri_ref, state_out, kick_out,
    state_ref, dest_ref, body_ref, code_ref,
    out1, got1, out2, sph, piece, sel_send, sel, names, names_got, names_smem,
    wide, point, plain, linear, coef0, coef1, coef2, coef3, slots0, slots1, sums, adds, order, order_smem, left, right, stacked, summed,
    part, part_got, row, row_got,
    s1, r1, s2, r2, t1s, t1r, ns, nr, t2s, t2r, w1s, w1r, w2s, w2r, own_sem, names_sem,
    in0, in1, in2, in3, in4,
):
    sector, bin_ = lax.axis_index("sector"), lax.axis_index("bin")
    inputs = [
        pltpu.make_async_copy(source, target, semaphore)
        for source, target, semaphore in (
            (dest_hbm, dest_ref, in0),
            (state_hbm, state_ref, in1),
            (body_hbm, body_ref, in2),
            (code_hbm, code_ref, in3),
        )
    ]
    for copy in inputs:
        copy.start()
    slots = (slots0, slots1)
    barrier = greet(sector, bin_)
    for copy in inputs:
        copy.wait()
    outgoing_tiles(state_ref, dest_ref, out1)
    lane = lax.broadcasted_iota(i32, (1, 128), 1)
    names[...] = jnp.where(lane == 0, body_ref[0, 0], body_ref[0, 1])
    set_adds(adds)
    for entry in range(2):
        slots[entry][32] = jnp.zeros((3, 128, 128), f32)
    set_order(code_ref, order)
    ordered = pltpu.make_async_copy(order, order_smem, in4)
    ordered.start()
    ordered.wait()
    pl.semaphore_wait(barrier, 2 * (N - 1))

    def along_sector(source, landing, sent, arrived):
        def copy(src, dst):
            return pltpu.make_async_remote_copy(
                src_ref=source(dst), dst_ref=landing(src), send_sem=sent, recv_sem=arrived,
                device_id=(dst, bin_), device_id_type=MESH,
            )

        return copy

    def along_bin(source, landing, sent, arrived):
        def copy(src, dst):
            return pltpu.make_async_remote_copy(
                src_ref=source(dst), dst_ref=landing(src), send_sem=sent, recv_sem=arrived,
                device_id=(sector, dst), device_id_type=MESH,
            )

        return copy

    def peers(me):
        return [lax.rem(me + off, N) for off in range(1, N)]

    def all_of(buffer, count, semaphore):
        view = buffer.at[pl.ds(0, count)]
        pltpu.make_async_copy(view, view, semaphore).wait()

    sphere_one = along_bin(lambda d: out1.at[d], lambda s: got1.at[s], s1, r1)
    sphere_two = along_sector(lambda d: out2.at[d], lambda s: sph.at[s], s2, r2)
    piece_one = along_sector(lambda d: tri_ref.at[pl.ds(3 * piece_of(d), 3)], lambda s: piece.at[s], t1s, t1r)
    names_one = along_sector(lambda d: names, lambda s: names_got.at[s], ns, nr)
    piece_two = along_sector(lambda d: sel_send.at[d], lambda s: sel.at[piece_of(s)], t2s, t2r)
    wrench_one = along_sector(lambda d: part.at[d], lambda s: part_got.at[s], w1s, w1r)
    wrench_two = along_bin(lambda d: row, lambda s: row_got.at[s], w2s, w2r)

    holding = is_holder(sector)
    for peer in peers(bin_):
        sphere_one(bin_, peer).start()
    for peer in peers(sector):

        @pl.when(is_holder(peer))
        def _(peer=peer):
            names_one(sector, peer).start()
            piece_one(sector, peer).start()

    @pl.when(holding)
    def _():
        own = pltpu.make_async_copy(tri_ref.at[pl.ds(3 * piece_of(sector), 3)], piece.at[sector], own_sem)
        own.start()
        names_got[sector] = names[...]
        own.wait()
        all_of(names_got, N - 1, nr)
        pltpu.make_async_copy(names_got, names_smem, names_sem).start()

    got1[bin_] = out1[bin_]
    all_of(got1, N - 1, r1)
    for ds, tile in enumerate(swap_groups([got1[sb] for sb in range(N)])):
        out2[ds] = tile
    for peer in peers(sector):
        sphere_two(sector, peer).start()
    sph[sector] = out2[sector]

    @pl.when(holding)
    def _():
        all_of(piece, N - 1, t1r)
        pltpu.make_async_copy(names_got, names_smem, names_sem).wait()
        for dst in range(N):
            for entry in range(2):
                sel_send[dst, entry] = piece[names_smem[dst, 0, entry]]
        for peer in peers(sector):
            piece_two(sector, peer).start()
        sel[piece_of(sector)] = sel_send[sector]

    all_of(sph, N - 1, r2)
    set_spheres(sph, wide, point)
    set_pairs(sph, left, right, stacked, summed)
    pair_sums(0, PAIRS_ONE, left, right, stacked, summed)

    @pl.when(holding)
    def _():
        all_of(sel, HOLDERS - 1, t2r)

    @pl.when(jnp.logical_not(holding))
    def _():
        all_of(sel, HOLDERS, t2r)

    set_triangles(sel, plain, linear)
    body_row = lax.broadcasted_iota(i32, (N, 1, 128), 0)
    parts = jnp.zeros((N, 1, 128), f32)
    wall_tiles(code_ref, plain, linear, wide, point, (coef0, coef1, coef2, coef3), slots, order_smem)
    for entry in range(2):
        parts = parts + jnp.where(body_row == body_ref[0, entry], wrench_line(entry, slots[entry], order_smem, wide)[None], 0.0)
    part[...] = parts

    for peer in peers(sector):
        wrench_one(sector, peer).start()
    part_got[sector] = part[sector]
    wall = wall_forces(slots, order_smem, sums, adds)
    pair_sums(PAIRS_ONE, PAIRS_TWO, left, right, stacked, summed)
    all_of(part_got, N - 1, w1r)
    row[...] = functools.reduce(jnp.add, [part_got[k] for k in range(N)])
    for peer in peers(bin_):
        wrench_two(bin_, peer).start()
    row_got[bin_] = row[...]
    pair_sums(PAIRS_TWO, PAIRS_ALL, left, right, stacked, summed)
    set_state(sph, summed, wall, state_out)
    all_of(row_got, N - 1, w2r)
    total = functools.reduce(jnp.add, [row_got[k] for k in range(N)])
    total = total * jnp.where(lane < 3, time_step / body_mass, time_step / body_inertia)
    kick_out[...] = total[:, 0:6]

    all_of(out1, N - 1, s1)
    all_of(out2, N - 1, s2)
    all_of(part, N - 1, w1s)
    all_of(row_got, N - 1, w2s)

    @pl.when(holding)
    def _():
        all_of(names_got, HOLDERS - 1, ns)
        all_of(piece, HOLDERS - 1, t1s)
        all_of(sel_send, N - 1, t2s)

    @pl.when(jnp.logical_not(holding))
    def _():
        all_of(names_got, HOLDERS, ns)
        all_of(piece, HOLDERS, t1s)


PAIRS_ONE, PAIRS_TWO, PAIRS_ALL = 1, 4, 8


def step(state, dest, bodies, codes, tri):
    slots = 2 * state.shape[1]
    vmem = pl.BlockSpec(memory_space=pltpu.VMEM)
    dma = pltpu.SemaphoreType.DMA
    line = pltpu.VMEM((N, 1, 128), f32)
    tiles = pltpu.VMEM((N, 8, 128), f32)
    return pl.pallas_call(
        step_kernel,
        out_shape=(pltpu.VMEM((7, slots), f32), pltpu.VMEM((1, 6), f32)),
        in_specs=[pl.BlockSpec(memory_space=pltpu.HBM)] * 5,
        out_specs=(vmem, vmem),
        scratch_shapes=[
            pltpu.VMEM(state.shape, f32),
            pltpu.VMEM(dest.shape, i32),
            pltpu.SMEM(bodies.shape, i32),
            pltpu.SMEM(codes.shape, i32),
            *[tiles] * 4,
            pltpu.VMEM((N, 3, 8, 128), f32),
            pltpu.VMEM((N, 2, 3, 8, 128), f32),
            pltpu.VMEM((HOLDERS, 2, 3, 8, 128), f32),
            pltpu.VMEM((1, 128), i32),
            pltpu.VMEM((N, 1, 128), i32),
            pltpu.SMEM((N, 1, 128), i32),
            pltpu.VMEM((N, 4, 128, 128), f32),
            pltpu.VMEM((N, 128, 48), bf16),
            pltpu.VMEM((2, 32, 16, 128), f32),
            pltpu.VMEM((2, 32, 8, 128), f32),
            *[pltpu.VMEM((128, 256), f32)] * 4,
            pltpu.VMEM((33, 3, 128, 128), f32),
            pltpu.VMEM((33, 3, 128, 128), f32),
            pltpu.VMEM((128, 128), f32),
            pltpu.VMEM((768, 128), bf16),
            pltpu.VMEM((4, 128), i32),
            pltpu.SMEM((4, 128), i32),
            pltpu.VMEM((slots, 32), bf16),
            pltpu.VMEM((32, slots), bf16),
            pltpu.VMEM((32, slots), bf16),
            pltpu.VMEM((32, slots), f32),
            line,
            line,
            pltpu.VMEM((1, 128), f32),
            line,
        ]
        + [dma] * 21,
        compiler_params=pltpu.CompilerParams(collective_id=0, has_side_effects=True, vmem_limit_bytes=60 * 2**20),
    )(state, dest, bodies, codes, tri)


def local(sph_state, sph_dest, body_list, tile_codes, triangles):
    dest = sph_dest.reshape(1, -1)
    tri = triangles.reshape(36, 8, 128)
    return step(sph_state, dest, body_list, tile_codes[0], tri)


def solution(mesh):
    return jax.shard_map(
        local,
        mesh=mesh,
        in_specs=(
            P(None, ("sector", "bin")),
            P(("sector", "bin"), None),
            P(("sector", "bin"), None),
            P(("sector", "bin"), None, None),
            P(None, "sector", "bin"),
        ),
        out_specs=(P(None, ("sector", "bin")), P("sector", None)),
        check_vma=False,
    )
```
